256 devices in a mesh: side: 2 (over core), grp: 16 (over x, y), shard: 8 (over z).
Axes of the slice: x: 4, y: 4, z: 8, core: 2. Of those that a mesh axis runs over, the one named last changes fastest.
Arguments:
- stream: bfloat16 [512, 4096], P(('side', 'shard'), 'grp'), may hold values from -9 to 9
- mixer_gain: float32 [4096], P('grp'), may hold values from 0.25 to 1.75
- in_weight: bfloat16 [4096, 2, 8192], P('grp', None, ('side', 'shard')), may hold values from -0.09375 to 0.09375
- conv_state: bfloat16 [512, 3, 8192], P('grp', None, ('side', 'shard')), may hold values from -6 to 6
- conv_weight: float32 [4, 8192], P(None, ('side', 'shard')), may hold values from -3 to 3
- conv_bias: float32 [8192], P(('side', 'shard')), may hold values from -3 to 3
- proj_weight: bfloat16 [544, 8192], P(None, ('side', 'shard')), may hold values from -0.0625 to 0.0625
- step_weight: bfloat16 [512, 8192], P(None, ('side', 'shard')), may hold values from -0.25 to 0.25
- step_bias: float32 [8192], P(('side', 'shard')), may hold values from -2 to 1
- decay_log: float32 [16, 8192], P(None, ('side', 'shard')), may hold values from -2 to 2.77
- skip_gain: float32 [8192], P(('side', 'shard')), may hold values from 0.1 to 1.9
- ssm_state: float32 [512, 16, 8192], P('grp', None, ('side', 'shard')), may hold values from -6 to 6
- out_weight: bfloat16 [8192, 4096], P(('side', 'shard'), 'grp'), may hold values from -0.0625 to 0.0625
- moe_gain: float32 [4096], P('grp'), may hold values from 0.25 to 1.75
- routes: int32 [512, 2], replicated, may hold values from 0 to 7, all different within a row; in each aligned block of 32 rows (0 to 31, 32 to 63, ...) at most 20 rows name the same one
- route_weight: float32 [512, 2], replicated, may hold values from 0.2 to 1
- gate_weight: bfloat16 [16, 4096, 6144], P('grp', None, ('side', 'shard')), may hold values from -0.09375 to 0.09375
- up_weight: bfloat16 [16, 4096, 6144], P('grp', None, ('side', 'shard')), may hold values from -0.09375 to 0.09375
- down_weight: bfloat16 [16, 6144, 4096], P('grp', ('side', 'shard')), may hold values from -0.0546875 to 0.0546875
Outputs:
- mixed: bfloat16 [512, 4096], P(('side', 'shard'), 'grp')
- new_state: float32 [512, 16, 8192], P('grp', None, ('side', 'shard'))
The draws below stay inside these ranges and needn't reach their ends.
Inputs may be any that keep to these rules, and one draw needn't show every extreme that they name: `routes`: each request names two different experts. In each aligned block of 32 requests (the requests of one device), no expert is named by more than 20 requests, a bound that some block reaches.
All inputs are finite; a program needn't handle non-finite values.
Results may differ from the reference program's by a relative error of at most 0.018.
Values may be sent and summed in bfloat16 or wider, within the bound.
No kernel may reach another device: no remote copies, remote signals or barrier semaphores. Data moves between devices by JAX's collectives and lax.ppermute only.
A program may use at most 128 MiB of HBM per device.

```python
import math
import jax
import jax.numpy as jnp
import numpy as np
from jax import lax

D = 4096
INNER = 8192
NSTATE = 16
RANK = 512
KCONV = 4
EXPERTS = 8
FF = 12288
REQ_DEV = 32
REQ = 512
CAP = 20


def draw_stream(key, part):
    key = jax.random.fold_in(key, 11)
    position = jnp.arange(D, dtype=jnp.float32) / (D - 1)
    values = jnp.clip(jax.random.normal(key, (REQ, D), jnp.float32), -6.0, 6.0)
    scale = 0.5 * jnp.power(3.0, position)
    return (values * scale[None, :]).astype(jnp.bfloat16)


def block_levels(stream_key, dims, shards, smallest, largest):
    level, own = 1.0, jax.random.fold_in(stream_key, 6)
    for dim, blocks in shards:
        draws = jnp.exp(jax.random.uniform(jax.random.fold_in(own, dim), (blocks,), jnp.float32, smallest / len(shards), largest / len(shards)))
        level = level * jnp.repeat(draws, dims[dim] // blocks).reshape([-1 if axis == dim else 1 for axis in range(len(dims))])
    return level


def assign_block(key, own, number, rows, count, top, bound, slope):
    order = jax.random.permutation(key, count)
    crowded, usual = load_shares(count, rows * top, bound, slope, True), load_shares(count, rows * top, bound, slope, False)
    places = jnp.arange(count)

    def named(sizes, rotation):
        used = int((sizes > 0).sum())
        fixed = max(1, used // 4)
        moved = fixed + (places - fixed + rotation * (used - fixed)) % max(1, count - fixed)
        return jnp.zeros((count,), jnp.int32).at[order[jnp.where(places < fixed, places, moved)]].set(jnp.asarray(sizes, jnp.int32))

    sizes = jnp.where(number % 4 == 0, named(crowded, number // 4), named(usual, number - number // 4 - 1))
    mixed = jax.random.permutation(jax.random.fold_in(own, 3), count)
    giver, sink = mixed[0:count // 2 * 2:2], mixed[1:count // 2 * 2:2]
    slack = jnp.minimum(sizes[giver] - 1, bound - sizes[sink]) // 2
    slack = jnp.where((giver == order[0]) | (sink == order[0]) | (sizes[sink] == 0), 0, jnp.maximum(slack, 0))
    moved = jax.random.randint(jax.random.fold_in(own, 4), (count // 2,), 0, 1 << 20) % (slack + 1)
    sizes = sizes.at[giver].add(-moved).at[sink].add(moved)
    labels = jnp.searchsorted(jnp.cumsum(sizes), jnp.arange(rows * top), side="right").astype(jnp.int32)
    listing = labels.reshape(top, rows).T
    listing = listing[jax.random.permutation(jax.random.fold_in(own, 1), rows)]
    rotation = jax.random.randint(jax.random.fold_in(own, 2), (rows, 1), 0, top)
    return jnp.take_along_axis(listing, (jnp.arange(top)[None, :] + rotation) % top, axis=1)


def load_shares(number_of, total, bound, lean, full):
    loads = [(1 << 20) // math.isqrt(standing ** lean) + 1 for standing in range(1, number_of + 1)]
    largest = bound if full else min(bound, max(-(-total // number_of), total * loads[0] // sum(loads)))
    least = 1 if total - largest >= number_of - 1 else 0
    holding, surplus = [largest] + [least] * (number_of - 1), total - largest - least * (number_of - 1)
    while surplus > 0:
        free = [i for i in range(1, number_of) if holding[i] < largest] or [i for i in range(1, number_of) if holding[i] < bound]
        mass, budget = sum([loads[i] for i in free]), surplus
        for i in free:
            extra = min(bound - holding[i], max(1, budget * loads[i] // mass), surplus)
            holding[i] = holding[i] + extra
            surplus = surplus - extra
    return np.array(holding)


def bell_draw(stream_key, extent, scale, reach, shards=(), kind=jnp.bfloat16):
    values = scale * jax.random.normal(stream_key, extent, jnp.float32)
    if shards:
        values = values * block_levels(stream_key, extent, shards, -0.22, 0.18)
    return jnp.clip(values, -reach, reach).astype(kind)


def setup_inputs(seed: int = 0) -> dict:
    arg_keys = jax.random.split(jax.random.key(seed), 20)
    stream = draw_stream(jax.random.fold_in(arg_keys[19], 71), 0)
    mixer_gain = jnp.clip(1.0 + 0.15 * jax.random.normal(arg_keys[1], (D,), jnp.float32), 0.25, 1.75)
    in_weight = bell_draw(arg_keys[2], (D, 2, INNER), D ** -0.5, 0.09375, ((0, 16), (2, 16)))
    conv_state = bell_draw(arg_keys[3], (REQ, KCONV - 1, INNER), 1.0, 6.0, ((0, 16), (2, 16)))
    conv_weight = bell_draw(arg_keys[4], (KCONV, INNER), 0.5, 3.0, ((1, 16),), jnp.float32)
    conv_bias = bell_draw(arg_keys[5], (INNER,), 0.5, 3.0, ((0, 16),), jnp.float32)
    proj_weight = bell_draw(arg_keys[6], (RANK + 2 * NSTATE, INNER), INNER ** -0.5, 0.0625, ((1, 16),))
    step_weight = bell_draw(arg_keys[7], (RANK, INNER), RANK ** -0.5, 0.25, ((1, 16),))
    step_bias = jnp.clip(-2.0 + 3.0 * jax.random.uniform(arg_keys[8], (INNER,), jnp.float32) ** block_levels(arg_keys[8], (INNER,), ((0, 16),), -0.2, 0.2), -2.0, 1.0)
    decay_log = jnp.clip(-2.0 + 4.77 * jax.random.uniform(arg_keys[9], (NSTATE, INNER), jnp.float32) ** block_levels(arg_keys[9], (NSTATE, INNER), ((1, 16),), -0.2, 0.2), -2.0, 2.77)
    skip_gain = jnp.clip(1.0 + 0.18 * jax.random.normal(arg_keys[10], (INNER,), jnp.float32), 0.1, 1.9)
    ssm_state = bell_draw(arg_keys[11], (REQ, NSTATE, INNER), 1.0, 6.0, ((0, 16), (2, 16)), jnp.float32)
    out_weight = bell_draw(arg_keys[12], (INNER, D), INNER ** -0.5, 0.0625, ((0, 16), (1, 16)))
    moe_gain = jnp.clip(1.0 + 0.15 * jax.random.normal(arg_keys[13], (D,), jnp.float32), 0.25, 1.75)
    routes_keys = jax.random.split(jax.random.fold_in(arg_keys[14], 1), REQ // REQ_DEV)
    routes_turns = jax.random.permutation(jax.random.fold_in(arg_keys[14], 3), REQ // REQ_DEV)
    routes = jax.vmap(lambda own, number: assign_block(jax.random.fold_in(arg_keys[14], 2), own, number, REQ_DEV, EXPERTS, 2, CAP, 2))(routes_keys, routes_turns).reshape((REQ, 2))
    route_weight = jnp.clip(jax.random.uniform(arg_keys[15], (REQ, 2), jnp.float32, 0.2, 1.0), 0.2, 1.0)
    gate_weight = bell_draw(arg_keys[16], (2 * EXPERTS, D, FF // 2), D ** -0.5, 0.09375, ((0, 16), (2, 16)))
    up_weight = bell_draw(arg_keys[17], (2 * EXPERTS, D, FF // 2), D ** -0.5, 0.09375, ((0, 16), (2, 16)))
    down_weight = bell_draw(arg_keys[18], (2 * EXPERTS, FF // 2, D), FF ** -0.5, 0.0546875, ((0, 16), (1, 16)))
    return dict(stream=stream, mixer_gain=mixer_gain, in_weight=in_weight, conv_state=conv_state, conv_weight=conv_weight, conv_bias=conv_bias, proj_weight=proj_weight, step_weight=step_weight, step_bias=step_bias, decay_log=decay_log, skip_gain=skip_gain, ssm_state=ssm_state, out_weight=out_weight, moe_gain=moe_gain, routes=routes, route_weight=route_weight, gate_weight=gate_weight, up_weight=up_weight, down_weight=down_weight)


def rms_norm(values, gain):
    wide = values.astype(jnp.float32)
    scale = lax.rsqrt(lax.optimization_barrier(jnp.mean(wide * wide, axis=-1, keepdims=True)) + 1e-06)
    return (wide * scale * gain).astype(jnp.bfloat16)

def reference(stream, mixer_gain, in_weight, conv_state, conv_weight, conv_bias, proj_weight, step_weight, step_bias, decay_log, skip_gain, ssm_state, out_weight, moe_gain, routes, route_weight, gate_weight, up_weight, down_weight):
    normed = rms_norm(stream, mixer_gain)
    projected = jnp.dot(normed, in_weight.reshape(D, 2 * INNER), preferred_element_type=jnp.float32).astype(jnp.bfloat16)
    x_in = projected[:, :INNER]
    gate_in = projected[:, INNER:]
    window = jnp.concatenate([conv_state, x_in[:, None, :]], axis=1).astype(jnp.float32)
    conv = lax.optimization_barrier(jnp.sum(window * conv_weight[None], axis=1)) + conv_bias
    activated = jax.nn.silu(conv).astype(jnp.bfloat16)
    params = lax.dot_general(activated, proj_weight, (((1,), (1,)), ((), ())), preferred_element_type=jnp.float32)
    low = params[:, :RANK].astype(jnp.bfloat16)
    entry = params[:, RANK:RANK + NSTATE]
    readout = params[:, RANK + NSTATE:]
    step = jax.nn.softplus(jnp.dot(low, step_weight, preferred_element_type=jnp.float32) + step_bias)
    act_wide = activated.astype(jnp.float32)
    decay = jnp.exp(-step[:, None, :] * jnp.exp(decay_log)[None])
    new_state = decay * ssm_state + (step * act_wide)[:, None, :] * entry[:, :, None]
    scanned = lax.optimization_barrier(jnp.sum(new_state * readout[:, :, None], axis=1)) + skip_gain * act_wide
    gated = (scanned * jax.nn.silu(gate_in.astype(jnp.float32))).astype(jnp.bfloat16)
    middle = stream.astype(jnp.float32) + jnp.dot(gated, out_weight, preferred_element_type=jnp.float32)
    moe_normed = rms_norm(middle, moe_gain)
    expert_ids = jnp.arange(EXPERTS, dtype=jnp.int32)
    matches = routes[:, :, None] == expert_ids[None, None, :]
    hits = lax.optimization_barrier(jnp.sum(matches.astype(jnp.int32), axis=1))
    weights = lax.optimization_barrier(jnp.sum(jnp.where(matches, route_weight[:, :, None], jnp.float32(0.0)), axis=1))
    slot_total = REQ // REQ_DEV * CAP

    def one_expert(total, expert):
        column = lax.dynamic_index_in_dim(hits, expert, 1, keepdims=False)
        rows_idx = jnp.nonzero(column > 0, size=slot_total, fill_value=0)[0].astype(jnp.int32)
        live = jnp.arange(slot_total, dtype=jnp.int32) < jnp.sum(column)
        rows = moe_normed[rows_idx]
        first = 2 * expert
        gate_full = jnp.concatenate([gate_weight[first], gate_weight[first + 1]], axis=1)
        up_full = jnp.concatenate([up_weight[first], up_weight[first + 1]], axis=1)
        down_full = jnp.concatenate([down_weight[first], down_weight[first + 1]], axis=0)
        gate = jnp.dot(rows, gate_full, preferred_element_type=jnp.float32)
        upper = jnp.dot(rows, up_full, preferred_element_type=jnp.float32)
        hidden = (jax.nn.silu(gate) * upper).astype(jnp.bfloat16)
        result = jnp.dot(hidden, down_full, preferred_element_type=jnp.float32).astype(jnp.bfloat16)
        weight_col = lax.dynamic_index_in_dim(weights, expert, 1, keepdims=False)
        row_weight = jnp.where(live, weight_col[rows_idx], jnp.float32(0.0))
        total = total.at[rows_idx].add(row_weight[:, None] * result.astype(jnp.float32))
        return (total, None)
    combined, unused = lax.scan(one_expert, jnp.zeros((REQ, D), jnp.float32), expert_ids)
    mixed = (middle + combined).astype(jnp.bfloat16)
    return (mixed, new_state)
```

```python
import jax
import jax.numpy as jnp
from jax import lax
from jax.sharding import PartitionSpec as P

D = 4096
NSTATE = 16
RANK = 512
EXPERTS = 8
CAP = 20
EPS = 1e-06
BF = jnp.bfloat16
F32 = jnp.float32


def spread(block, axis):
    count = lax.axis_size(axis)
    return lax.all_to_all(jnp.broadcast_to(block[None], (count,) + block.shape), axis, 0, 0)


def swap(block):
    return lax.ppermute(block, "side", [(0, 1), (1, 0)])


def in_order(side, own, other):
    first = side == 0
    return jnp.stack([jnp.where(first, own, other), jnp.where(first, other, own)])


def pick(pair, index):
    return lax.dynamic_index_in_dim(pair, index, 0, keepdims=False)


def split_wide(values):
    high = values.astype(BF)
    low = (values - high.astype(F32)).astype(BF)
    return high, low


def slot_tables(routes, weights):
    expert_ids = jnp.arange(EXPERTS, dtype=jnp.int32)
    slot_ids = jnp.arange(CAP, dtype=jnp.int32)
    matches = routes[:, :, :, None] == expert_ids
    hits = jnp.sum(matches.astype(jnp.int32), axis=2)
    slots = jnp.cumsum(hits, axis=1) - 1
    mixing = jnp.sum(jnp.where(matches, weights[:, :, :, None], F32(0.0)), axis=2)
    place = jnp.where(hits == 1, slots, -1).transpose(0, 2, 1)
    select = place[:, :, None, :] == slot_ids[None, None, :, None]
    slot_weights = jnp.sum(jnp.where(select, mixing.transpose(0, 2, 1)[:, :, None, :], F32(0.0)), axis=3)
    return select, slot_weights


def local(
    stream,
    mixer_gain,
    in_weight,
    conv_state,
    conv_weight,
    conv_bias,
    proj_weight,
    step_weight,
    step_bias,
    decay_log,
    skip_gain,
    ssm_state,
    out_weight,
    moe_gain,
    routes,
    route_weight,
    gate_weight,
    up_weight,
    down_weight,
):
    side = lax.axis_index("side")
    grp = lax.axis_index("grp")
    groups = lax.axis_size("grp")
    shards = lax.axis_size("shard")
    rows, slice_width = stream.shape
    width = in_weight.shape[2]
    side_rows = shards * rows

    near = spread(stream, "shard")
    far = swap(near)
    whole = in_order(side, near, far).reshape(2 * side_rows, slice_width).astype(F32)
    squares = jnp.sum(whole * whole, axis=1)
    scaled = (whole * mixer_gain).astype(BF)

    part = jnp.dot(scaled, in_weight.reshape(slice_width, 2 * width), preferred_element_type=F32)
    high, low = split_wide(squares)
    extra = jnp.pad(jnp.stack([high, low], axis=1), ((0, 0), (0, 126)))
    packet = jnp.concatenate([part.astype(BF), extra], axis=1).reshape(groups, rows, 2 * width + 128)
    total = jnp.sum(lax.all_to_all(packet, "grp", 0, 0).astype(F32), axis=0)
    scale = lax.rsqrt((total[:, 2 * width] + total[:, 2 * width + 1]) / D + EPS)
    projected = (total[:, : 2 * width] * scale[:, None]).astype(BF)
    x_in = projected[:, :width]
    gate_in = projected[:, width:]

    window = jnp.concatenate([conv_state, x_in[:, None, :]], axis=1).astype(F32)
    conv = jnp.sum(window * conv_weight[None], axis=1) + conv_bias
    activated = jax.nn.silu(conv).astype(BF)

    part = lax.dot_general(activated, proj_weight, (((1,), (1,)), ((), ())), preferred_element_type=F32)
    pair = part.reshape(2, rows // 2, part.shape[1])
    half = pick(pair, side) + swap(pick(pair, 1 - side))
    half = jnp.sum(spread(half.astype(BF), "shard").astype(F32), axis=0)
    params = in_order(side, half, swap(half)).reshape(rows, part.shape[1])

    low = params[:, :RANK].astype(BF)
    entry = params[:, RANK : RANK + NSTATE]
    readout = params[:, RANK + NSTATE :]
    step = jax.nn.softplus(jnp.dot(low, step_weight, preferred_element_type=F32) + step_bias)
    act_wide = activated.astype(F32)
    decay = jnp.exp(-step[:, None, :] * jnp.exp(decay_log)[None])
    new_state = decay * ssm_state + (step * act_wide)[:, None, :] * entry[:, :, None]
    scanned = jnp.sum(new_state * readout[:, :, None], axis=1) + skip_gain * act_wide
    gated = (scanned * jax.nn.silu(gate_in.astype(F32))).astype(BF)

    all_gated = spread(gated, "grp").reshape(groups * rows, width)
    part = jnp.dot(all_gated, out_weight, preferred_element_type=F32).reshape(2, side_rows, slice_width)
    half = pick(part, side) + swap(pick(part, 1 - side).astype(BF)).astype(F32)
    packet = half.astype(BF).reshape(shards, rows, slice_width)
    mixer_out = jnp.sum(lax.all_to_all(packet, "shard", 0, 0).astype(F32), axis=0)
    middle = stream.astype(F32) + mixer_out

    dense = spread((middle * moe_gain).astype(BF), "shard")
    plain = dense.astype(F32) / moe_gain
    squares = jnp.sum(plain * plain, axis=2)
    select, slot_weights = slot_tables(
        routes.reshape(2 * shards, rows, 2), route_weight.reshape(2 * shards, rows, 2)
    )
    mine = lax.dynamic_slice_in_dim(select, side * shards, shards, 0)
    slots = shards * CAP
    picked = jnp.einsum("becr,brf->ebcf", mine.astype(BF), dense, preferred_element_type=F32).astype(BF)
    picked = picked.reshape(EXPERTS, slots, slice_width)
    slot_squares = jnp.sum(jnp.where(mine, squares[:, None, None, :], F32(0.0)), axis=3)
    slot_squares = slot_squares.transpose(1, 0, 2).reshape(EXPERTS, slots)
    high, low = split_wide(slot_squares)
    extra = jnp.pad(jnp.stack([high, low], axis=1), ((0, 0), (0, 14), (0, slice_width - slots)))
    packet = jnp.repeat(jnp.concatenate([picked, extra], axis=1), 2, axis=0)
    near = lax.all_to_all(packet, "grp", 0, 0)
    far = swap(near)
    both = jnp.concatenate([near[:, :slots], far[:, :slots]], axis=1)
    tail = jnp.stack([near[:, slots : slots + 2, :slots], far[:, slots : slots + 2, :slots]]).astype(F32)
    scale = lax.rsqrt(jnp.sum(tail, axis=(1, 2)).reshape(2 * slots, 1) / D + EPS)

    shape = (groups, slice_width, gate_weight.shape[2])
    gate = jnp.einsum("srf,sfk->rk", both, gate_weight.reshape(shape), preferred_element_type=F32)
    upper = jnp.einsum("srf,sfk->rk", both, up_weight.reshape(shape), preferred_element_type=F32)
    hidden = (jax.nn.silu(gate * scale) * (upper * scale)).astype(BF)
    own_weights = lax.dynamic_index_in_dim(slot_weights, grp // 2, 1, keepdims=False).reshape(2, slots)
    own_weights = jnp.concatenate([pick(own_weights, side), pick(own_weights, 1 - side)])
    part = jnp.dot(hidden, down_weight[0], preferred_element_type=F32) * own_weights[:, None]
    part = part.reshape(2, slots, groups, slice_width).transpose(0, 2, 1, 3)
    packet = (part[0] + swap(part[1].astype(BF)).astype(F32)).astype(BF)
    back = lax.all_to_all(packet, "grp", 0, 0)

    back = back.reshape(EXPERTS, 2, shards, CAP, slice_width)
    part = jnp.einsum("becr,ehbcf->brf", mine.astype(BF), back, preferred_element_type=F32)
    moe_out = jnp.sum(lax.all_to_all(part.astype(BF), "shard", 0, 0).astype(F32), axis=0)
    mixed = (middle + moe_out).astype(BF)
    return (mixed, new_state)


def solution(mesh):
    placed = (
        P(("side", "shard"), "grp"),
        P("grp"),
        P("grp", None, ("side", "shard")),
        P("grp", None, ("side", "shard")),
        P(None, ("side", "shard")),
        P(("side", "shard")),
        P(None, ("side", "shard")),
        P(None, ("side", "shard")),
        P(("side", "shard")),
        P(None, ("side", "shard")),
        P(("side", "shard")),
        P("grp", None, ("side", "shard")),
        P(("side", "shard"), "grp"),
        P("grp"),
        P(),
        P(),
        P("grp", None, ("side", "shard")),
        P("grp", None, ("side", "shard")),
        P("grp", ("side", "shard"), None),
    )
    return jax.shard_map(
        local,
        mesh=mesh,
        in_specs=placed,
        out_specs=(P(("side", "shard"), "grp"), P("grp", None, ("side", "shard"))),
        check_vma=False,
    )
```

```python
import jax
import jax.numpy as jnp
from jax import lax
from jax.experimental import pallas as pl
from jax.experimental.pallas import tpu as pltpu
from jax.sharding import PartitionSpec as P

D = 4096
NSTATE = 16
RANK = 512
EXPERTS = 8
CAP = 20
EPS = 1e-06
BF = jnp.bfloat16
F32 = jnp.float32


def on_core(kernel, outs, *operands, limit=24, flops=0):
    vmem = pl.BlockSpec(memory_space=pltpu.VMEM)
    moved = sum(o.size * o.dtype.itemsize for o in operands)
    return pl.pallas_call(
        kernel,
        out_shape=[jax.ShapeDtypeStruct(s, d) for s, d in outs],
        in_specs=[vmem] * len(operands),
        out_specs=[vmem] * len(outs),
        compiler_params=pltpu.CompilerParams(vmem_limit_bytes=limit * 2**20),
        cost_estimate=pl.CostEstimate(flops=flops, bytes_accessed=moved, transcendentals=0),
    )(*operands)


def dot(a, b):
    return jnp.dot(a, b, preferred_element_type=F32)


def split_wide(values):
    high = values.astype(BF)
    low = (values - high.astype(F32)).astype(BF)
    return high, low


def swap(block):
    return lax.ppermute(block, "side", [(0, 1), (1, 0)])


def exchange(block, axis):
    return lax.all_to_all(block, axis, 0, 0)


def spread(block, axis):
    count = lax.axis_size(axis)
    return exchange(jnp.broadcast_to(block[None], (count,) + block.shape), axis)


def pick(pair, index):
    return lax.dynamic_index_in_dim(pair, index, 0, keepdims=False)


def project_kernel(x_ref, gain_ref, w_ref, tail_ref, out_ref):
    shards, sides, rows, depth = x_ref.shape
    width = w_ref.shape[1]
    lane = lax.broadcasted_iota(jnp.int32, (rows, 128), 1)
    for c in range(sides):
        wide = x_ref[:, c].reshape(shards * rows, depth).astype(F32)
        squares = jnp.sum(wide * wide, axis=1, keepdims=True)
        part = dot((wide * gain_ref[...]).astype(BF), w_ref[...])
        for z in range(shards):
            span = slice(z * rows, (z + 1) * rows)
            out_ref[c * shards + z, :, :width] = part[span].astype(BF)
            high = squares[span].astype(BF).astype(F32)
            low = squares[span] - high
            extra = jnp.where(lane == 0, high, jnp.where(lane == 1, low, tail_ref[...]))
            out_ref[c * shards + z, :, width:] = extra.astype(BF)


def conv_kernel(x_ref, state_ref, taps_ref, bias_ref, proj_ref, act_ref, gate_ref, part_ref):
    width = act_ref.shape[1]
    total = jnp.sum(x_ref[...].astype(F32), axis=0)
    scale = lax.rsqrt((total[:, 2 * width : 2 * width + 1] + total[:, 2 * width + 1 : 2 * width + 2]) / D + EPS)
    newest = (total[:, :width] * scale).astype(BF).astype(F32)
    gate = (total[:, width : 2 * width] * scale).astype(BF).astype(F32)
    conv = newest * taps_ref[3:4, :]
    for k in range(3):
        conv = conv + state_ref[k].astype(F32) * taps_ref[k : k + 1, :]
    activated = jax.nn.silu(conv + bias_ref[...]).astype(BF)
    act_ref[...] = activated
    gate_ref[...] = jax.nn.silu(gate)
    part_ref[...] = lax.dot_general(
        activated, proj_ref[...], (((1,), (1,)), ((), ())), preferred_element_type=F32
    )


def join_kernel(a_ref, b_ref, out_ref):
    joined = (a_ref[...] + b_ref[...]).astype(BF)
    for z in range(out_ref.shape[0]):
        out_ref[z] = joined


def mixer_out_kernel(side_ref, x_ref, w_ref, own_ref, other_ref):
    groups, rows, width = x_ref.shape
    half = groups // 2
    side = side_ref[0]
    other = x_ref[pl.ds((1 - side) * half, half)].reshape(half * rows, width)
    other_ref[...] = dot(other, w_ref[...]).astype(BF)
    own = x_ref[pl.ds(side * half, half)].reshape(half * rows, width)
    own_ref[...] = dot(own, w_ref[...])


def add_kernel(a_ref, b_ref, out_ref):
    joined = a_ref[...] + b_ref[...].astype(F32)
    out_ref[...] = joined.astype(BF).reshape(out_ref.shape)


def middle_kernel(x_ref, stream_ref, gain_ref, middle_ref, out_ref):
    middle = stream_ref[...].astype(F32) + jnp.sum(x_ref[...].astype(F32), axis=0)
    middle_ref[...] = middle
    scaled = (middle * gain_ref[...]).astype(BF)
    for z in range(out_ref.shape[0]):
        out_ref[z] = scaled


def dispatch_kernel(x_ref, select_ref, out_ref):
    shards, rows, depth = x_ref.shape
    dense = x_ref[...].reshape(shards * rows, depth)
    for e in range(EXPERTS):
        picked = dot(select_ref[e], dense).astype(BF)
        out_ref[2 * e] = picked
        out_ref[2 * e + 1] = picked


def expert_kernel(x_ref, inverse_ref, slot_ref, g_ref, u_ref, d_ref, *refs):
    add_ref, out_ref = refs if len(refs) == 2 else (None, refs[0])
    groups, slots, depth = x_ref.shape
    gate = jnp.zeros((slots, g_ref.shape[1]), F32)
    upper = jnp.zeros((slots, g_ref.shape[1]), F32)
    squares = jnp.zeros((slots, 1), F32)
    for s in range(groups):
        span = slice(s * depth, (s + 1) * depth)
        block = x_ref[s]
        gate = gate + dot(block, g_ref[span, :])
        upper = upper + dot(block, u_ref[span, :])
        plain = block.astype(F32) * inverse_ref[s : s + 1, :]
        squares = squares + jnp.sum(plain * plain, axis=1, keepdims=True)
    scale = lax.rsqrt(squares / D + EPS)
    hidden = (jax.nn.silu(gate * scale) * (upper * scale)).astype(BF)
    for s in range(groups):
        span = slice(s * depth, (s + 1) * depth)
        part = dot(hidden, d_ref[:, span]) * slot_ref[...]
        if add_ref is not None:
            part = part + add_ref[s].astype(F32)
        out_ref[s] = part.astype(BF)


def combine_kernel(x_ref, select_ref, out_ref):
    shards, rows, depth = out_ref.shape
    total = jnp.zeros((shards * rows, depth), F32)
    for e in range(EXPERTS):
        total = total + dot(select_ref[e], x_ref[2 * e])
        total = total + dot(select_ref[e], x_ref[2 * e + 1])
    out_ref[...] = total.astype(BF).reshape(shards, rows, depth)


def final_kernel(x_ref, middle_ref, out_ref):
    out_ref[...] = (middle_ref[...] + jnp.sum(x_ref[...].astype(F32), axis=0)).astype(BF)


def slot_tables(routes, weights):
    expert_ids = jnp.arange(EXPERTS, dtype=jnp.int32)
    slot_ids = jnp.arange(CAP, dtype=jnp.int32)
    matches = routes[:, :, :, None] == expert_ids
    hits = jnp.sum(matches.astype(jnp.int32), axis=2)
    slots = jnp.cumsum(hits, axis=1) - 1
    mixing = jnp.sum(jnp.where(matches, weights[:, :, :, None], F32(0.0)), axis=2)
    place = jnp.where(hits == 1, slots, -1).transpose(0, 2, 1)
    select = place[:, :, None, :] == slot_ids[None, None, :, None]
    slot_weights = jnp.sum(jnp.where(select, mixing.transpose(0, 2, 1)[:, :, None, :], F32(0.0)), axis=3)
    return select, slot_weights


def local(
    stream,
    mixer_gain,
    in_weight,
    conv_state,
    conv_weight,
    conv_bias,
    proj_weight,
    step_weight,
    step_bias,
    decay_log,
    skip_gain,
    ssm_state,
    out_weight,
    moe_gain,
    routes,
    route_weight,
    gate_weight,
    up_weight,
    down_weight,
):
    side = lax.axis_index("side")
    grp = lax.axis_index("grp")
    groups = lax.axis_size("grp")
    shards = lax.axis_size("shard")
    rows, slice_width = stream.shape
    width = in_weight.shape[2]
    side_rows = shards * rows
    slots = shards * CAP

    high, rest = split_wide(moe_gain)
    mid = (moe_gain - high.astype(F32) - rest.astype(F32)).astype(BF)
    lanes = slice_width // rows
    tail = jnp.concatenate([t.reshape(rows, lanes) for t in (high, rest, mid)], axis=1).astype(F32)
    tail = jnp.pad(tail, ((0, 0), (2, 126 - 3 * lanes)))

    own = stream
    other = swap(stream)
    first = side == 0
    pair = jnp.stack([jnp.where(first, own, other), jnp.where(first, other, own)])
    whole = spread(pair, "shard")

    (packet,) = on_core(
        project_kernel,
        [((groups, rows, 2 * width + 128), BF)],
        whole,
        mixer_gain[None],
        in_weight.reshape(slice_width, 2 * width),
        tail,
    )
    arrived = exchange(packet, "grp")
    activated, gate, part = on_core(
        conv_kernel,
        [((rows, width), BF), ((rows, width), F32), ((rows, proj_weight.shape[0]), F32)],
        arrived,
        conv_state.transpose(1, 0, 2),
        conv_weight,
        conv_bias[None],
        proj_weight,
    )
    gains = arrived[:, :, 2 * width + 2 : 2 * width + 2 + 3 * lanes].astype(F32)
    gains = jnp.sum(gains.reshape(groups, rows, 3, lanes), axis=2).reshape(groups, slice_width)
    inverse = 1.0 / gains

    (packet,) = on_core(join_kernel, [((shards,) + part.shape, BF)], part, swap(part))
    params = jnp.sum(exchange(packet, "shard").astype(F32), axis=0)

    low = params[:, :RANK].astype(BF)
    entry = params[:, RANK : RANK + NSTATE]
    readout = params[:, RANK + NSTATE :]
    step = jax.nn.softplus(dot(low, step_weight) + step_bias)
    act_wide = activated.astype(F32)
    decay = jnp.exp(-step[:, None, :] * jnp.exp(decay_log)[None])
    new_state = decay * ssm_state + (step * act_wide)[:, None, :] * entry[:, :, None]
    scanned = jnp.sum(new_state * readout[:, :, None], axis=1) + skip_gain * act_wide
    gated = (scanned * gate).astype(BF)

    all_gated = spread(gated, "grp")
    vmem = pl.BlockSpec(memory_space=pltpu.VMEM)
    own, other = pl.pallas_call(
        mixer_out_kernel,
        out_shape=[
            jax.ShapeDtypeStruct((side_rows, slice_width), F32),
            jax.ShapeDtypeStruct((side_rows, slice_width), BF),
        ],
        in_specs=[pl.BlockSpec(memory_space=pltpu.SMEM), vmem, vmem],
        out_specs=[vmem, vmem],
    )(side.astype(jnp.int32).reshape(1), all_gated, out_weight)
    (packet,) = on_core(add_kernel, [((shards, rows, slice_width), BF)], own, swap(other))
    middle, packet = on_core(
        middle_kernel,
        [((rows, slice_width), F32), ((shards, rows, slice_width), BF)],
        exchange(packet, "shard"),
        stream,
        moe_gain[None],
    )
    dense = exchange(packet, "shard")

    select, slot_weights = slot_tables(
        routes.reshape(2 * shards, rows, 2), route_weight.reshape(2 * shards, rows, 2)
    )
    mine = lax.dynamic_slice_in_dim(select, side * shards, shards, 0)
    same = jnp.eye(shards, dtype=jnp.bool_)
    pick_rows = mine.transpose(1, 0, 2, 3)[:, :, :, None, :] & same[None, :, None, :, None]
    pick_rows = pick_rows.reshape(EXPERTS, slots, side_rows).astype(BF)
    place_rows = mine.transpose(1, 0, 3, 2)[:, :, :, None, :] & same[None, :, None, :, None]
    place_rows = place_rows.reshape(EXPERTS, side_rows, slots).astype(BF)
    own_weights = lax.dynamic_index_in_dim(slot_weights, grp // 2, 1, keepdims=False).reshape(2, slots, 1)

    (packet,) = on_core(dispatch_kernel, [((groups, slots, slice_width), BF)], dense, pick_rows)
    near = exchange(packet, "grp")
    far = swap(near)

    weights = (gate_weight[0], up_weight[0], down_weight[0])
    shape = [((groups, slots, slice_width), BF)]
    work = 2 * slots * D * 3 * gate_weight.shape[2]
    (other,) = on_core(
        expert_kernel, shape, far, inverse, pick(own_weights, 1 - side), *weights, limit=40, flops=work
    )
    (packet,) = on_core(
        expert_kernel, shape, near, inverse, pick(own_weights, side), *weights, swap(other), limit=40, flops=work
    )
    back = exchange(packet, "grp")

    (packet,) = on_core(combine_kernel, [((shards, rows, slice_width), BF)], back, place_rows)
    (mixed,) = on_core(final_kernel, [((rows, slice_width), BF)], exchange(packet, "shard"), middle)
    return (mixed, new_state)


def solution(mesh):
    placed = (
        P(("side", "shard"), "grp"),
        P("grp"),
        P("grp", None, ("side", "shard")),
        P("grp", None, ("side", "shard")),
        P(None, ("side", "shard")),
        P(("side", "shard")),
        P(None, ("side", "shard")),
        P(None, ("side", "shard")),
        P(("side", "shard")),
        P(None, ("side", "shard")),
        P(("side", "shard")),
        P("grp", None, ("side", "shard")),
        P(("side", "shard"), "grp"),
        P("grp"),
        P(),
        P(),
        P("grp", None, ("side", "shard")),
        P("grp", None, ("side", "shard")),
        P("grp", ("side", "shard"), None),
    )
    return jax.shard_map(
        local,
        mesh=mesh,
        in_specs=placed,
        out_specs=(P(("side", "shard"), "grp"), P("grp", None, ("side", "shard"))),
        check_vma=False,
    )
```

```python
import jax
import jax.numpy as jnp
from jax import lax
from jax.experimental import pallas as pl
from jax.experimental.pallas import tpu as pltpu
from jax.sharding import PartitionSpec as P

D = 4096
NSTATE = 16
RANK = 512
EXPERTS = 8
CAP = 20
REQ_DEV = 32
EPS = 1e-06
BF = jnp.bfloat16
F32 = jnp.float32


def on_core(kernel, outs, *operands, limit=24, flops=0):
    vmem = pl.BlockSpec(memory_space=pltpu.VMEM)
    moved = sum(o.size * o.dtype.itemsize for o in operands)
    return pl.pallas_call(
        kernel,
        out_shape=[jax.ShapeDtypeStruct(s, d) for s, d in outs],
        in_specs=[vmem] * len(operands),
        out_specs=[vmem] * len(outs),
        compiler_params=pltpu.CompilerParams(vmem_limit_bytes=limit * 2**20),
        cost_estimate=pl.CostEstimate(flops=flops, bytes_accessed=moved, transcendentals=0),
    )(*operands)


def dot(a, b):
    return jnp.dot(a, b, preferred_element_type=F32)


def split_wide(values):
    high = values.astype(BF)
    low = (values - high.astype(F32)).astype(BF)
    return high, low


def swap(block):
    return lax.ppermute(block, "side", [(0, 1), (1, 0)])


def exchange(block, axis):
    return lax.all_to_all(block, axis, 0, 0)


def spread(block, axis):
    count = lax.axis_size(axis)
    return exchange(jnp.broadcast_to(block[None], (count,) + block.shape), axis)


def project_kernel(near_ref, far_ref, gain_ref, w_ref, tail_ref, out_ref):
    shards, rows, depth = near_ref.shape
    width = w_ref.shape[1]
    side = lax.axis_index("side")
    lane = lax.broadcasted_iota(jnp.int32, (rows, 128), 1)
    for x_ref, c in ((near_ref, side), (far_ref, 1 - side)):
        wide = x_ref[...].reshape(shards * rows, depth).astype(F32)
        squares = jnp.sum(wide * wide, axis=1, keepdims=True)
        part = dot((wide * gain_ref[...]).astype(BF), w_ref[...])
        for z in range(shards):
            span = slice(z * rows, (z + 1) * rows)
            out_ref[c * shards + z, :, :width] = part[span].astype(BF)
            high = squares[span].astype(BF).astype(F32)
            low = squares[span] - high
            extra = jnp.where(lane == 0, high, jnp.where(lane == 1, low, tail_ref[...]))
            out_ref[c * shards + z, :, width:] = extra.astype(BF)


def conv_kernel(x_ref, state_ref, taps_ref, bias_ref, proj_ref, act_ref, gate_ref, own_ref, other_ref):
    width = act_ref.shape[1]
    total = jnp.sum(x_ref[...].astype(F32), axis=0)
    scale = lax.rsqrt((total[:, 2 * width : 2 * width + 1] + total[:, 2 * width + 1 : 2 * width + 2]) / D + EPS)
    newest = (total[:, :width] * scale).astype(BF).astype(F32)
    gate = (total[:, width : 2 * width] * scale).astype(BF).astype(F32)
    conv = newest * taps_ref[3:4, :]
    for k in range(3):
        conv = conv + state_ref[k].astype(F32) * taps_ref[k : k + 1, :]
    activated = jax.nn.silu(conv + bias_ref[...]).astype(BF)
    act_ref[...] = activated
    gate_ref[...] = jax.nn.silu(gate)
    part = lax.dot_general(
        activated, proj_ref[...], (((1,), (1,)), ((), ())), preferred_element_type=F32
    )
    half = part.shape[0] // 2
    first = lax.axis_index("side") == 0
    own_ref[...] = jnp.where(first, part[:half], part[half:])
    other_ref[...] = jnp.where(first, part[half:], part[:half])


def join_kernel(a_ref, b_ref, out_ref):
    joined = (a_ref[...] + b_ref[...]).astype(BF)
    for z in range(out_ref.shape[0]):
        out_ref[z] = joined


def mixer_out_kernel(x_ref, w_ref, own_ref, other_ref):
    groups, rows, width = x_ref.shape
    half = groups // 2
    side = lax.axis_index("side")
    other = x_ref[pl.ds((1 - side) * half, half)].reshape(half * rows, width)
    other_ref[...] = dot(other, w_ref[...]).astype(BF)
    own = x_ref[pl.ds(side * half, half)].reshape(half * rows, width)
    own_ref[...] = dot(own, w_ref[...])


def add_kernel(a_ref, b_ref, out_ref):
    joined = a_ref[...] + b_ref[...].astype(F32)
    out_ref[...] = joined.astype(BF).reshape(out_ref.shape)


def middle_kernel(x_ref, stream_ref, gain_ref, middle_ref, out_ref):
    middle = stream_ref[...].astype(F32) + jnp.sum(x_ref[...].astype(F32), axis=0)
    middle_ref[...] = middle
    scaled = (middle * gain_ref[...]).astype(BF)
    for z in range(out_ref.shape[0]):
        out_ref[z] = scaled


def tables_kernel(routes_ref, weights_ref, column_ref, place_ref, mixing_ref, place_t_ref):
    requests = routes_ref.shape[1]
    block = REQ_DEV
    half = requests // 2
    early = lax.broadcasted_iota(jnp.int32, (requests, requests), 0)
    late = lax.broadcasted_iota(jnp.int32, (requests, requests), 1)
    shared = early // block == late // block
    upto = (shared & (early <= late)).astype(F32).astype(BF)
    since = (shared & (early >= late)).astype(F32).astype(BF)

    expert = lax.broadcasted_iota(jnp.int32, (EXPERTS, requests), 0)
    one = routes_ref[0:1, :] == expert
    two = routes_ref[1:2, :] == expert
    mixing_ref[...] = jnp.where(one, weights_ref[0:1, :], F32(0.0)) + jnp.where(two, weights_ref[1:2, :], F32(0.0))
    hits = (one | two).astype(F32)
    slot = dot(hits.astype(BF), upto).astype(jnp.int32) - 1
    request = lax.broadcasted_iota(jnp.int32, (EXPERTS, requests), 1)
    place_ref[...] = jnp.where(one | two, slot + (request % half) // block * CAP, -1)

    expert = lax.broadcasted_iota(jnp.int32, (requests, 128), 1)
    hit = (column_ref[:, 0:1] == expert) | (column_ref[:, 1:2] == expert)
    slot = dot(since, hit.astype(F32).astype(BF)).astype(jnp.int32) - 1
    request = lax.broadcasted_iota(jnp.int32, (requests, 128), 0)
    place_t_ref[...] = jnp.where(hit, slot + (request % half) // block * CAP, -1)


def dispatch_kernel(x_ref, place_ref, out_ref):
    shards, rows, depth = x_ref.shape
    slots = out_ref.shape[1]
    dense = x_ref[...].reshape(shards * rows, depth)
    place = jnp.where(lax.axis_index("side") == 0, place_ref[:, : shards * rows], place_ref[:, shards * rows :])
    slot = lax.broadcasted_iota(jnp.int32, (slots, shards * rows), 0)
    for e in range(EXPERTS):
        select = (slot == place[e : e + 1, :]).astype(F32).astype(BF)
        picked = dot(select, dense).astype(BF)
        out_ref[2 * e] = picked
        out_ref[2 * e + 1] = picked


def expert_hidden(x_ref, inverse_ref, g_ref, u_ref):
    groups, slots, depth = x_ref.shape
    gate = jnp.zeros((slots, g_ref.shape[2]), F32)
    upper = jnp.zeros((slots, g_ref.shape[2]), F32)
    squares = jnp.zeros((slots, 1), F32)
    for s in range(groups):
        span = slice(s * depth, (s + 1) * depth)
        block = x_ref[s]
        gate = gate + dot(block, g_ref[0, span, :])
        upper = upper + dot(block, u_ref[0, span, :])
        plain = block.astype(F32) * inverse_ref[s : s + 1, :]
        squares = squares + jnp.sum(plain * plain, axis=1, keepdims=True)
    scale = lax.rsqrt(squares / D + EPS)
    return (jax.nn.silu(gate * scale) * (upper * scale)).astype(BF)


def slot_weight(slots, place_ref, mixing_ref, far):
    half = place_ref.shape[1] // 2
    expert = lax.axis_index("grp") // 2
    low_half = (lax.axis_index("side") == 0) != far
    row = lax.broadcasted_iota(jnp.int32, place_ref.shape, 0) == expert
    place = jnp.sum(jnp.where(row, place_ref[...], 0), axis=0, keepdims=True)
    mixing = jnp.sum(jnp.where(row, mixing_ref[...], F32(0.0)), axis=0, keepdims=True)
    place = jnp.where(low_half, place[:, :half], place[:, half:])
    mixing = jnp.where(low_half, mixing[:, :half], mixing[:, half:])
    slot = lax.broadcasted_iota(jnp.int32, (slots, half), 0)
    return jnp.sum(jnp.where(slot == place, mixing, F32(0.0)), axis=1, keepdims=True)


def near_hidden_kernel(x_ref, inverse_ref, g_ref, u_ref, out_ref):
    out_ref[...] = expert_hidden(x_ref, inverse_ref, g_ref, u_ref)


def far_kernel(x_ref, inverse_ref, place_ref, mixing_ref, g_ref, u_ref, d_ref, out_ref):
    groups, slots, depth = out_ref.shape
    hidden = expert_hidden(x_ref, inverse_ref, g_ref, u_ref)
    weight = slot_weight(slots, place_ref, mixing_ref, True)
    for s in range(groups):
        out_ref[s] = (dot(hidden, d_ref[0, :, s * depth : (s + 1) * depth]) * weight).astype(BF)


def near_down_kernel(hidden_ref, place_ref, mixing_ref, d_ref, add_ref, out_ref):
    groups, slots, depth = out_ref.shape
    hidden = hidden_ref[...]
    weight = slot_weight(slots, place_ref, mixing_ref, False)
    for s in range(groups):
        part = dot(hidden, d_ref[0, :, s * depth : (s + 1) * depth]) * weight
        out_ref[s] = (part + add_ref[s].astype(F32)).astype(BF)


def combine_kernel(x_ref, place_ref, out_ref):
    shards, rows, depth = out_ref.shape
    slots = x_ref.shape[1]
    half = shards * rows
    place = jnp.where(lax.axis_index("side") == 0, place_ref[:half, :], place_ref[half:, :])
    slot = lax.broadcasted_iota(jnp.int32, (half, slots), 1)
    total = jnp.zeros((half, depth), F32)
    for e in range(EXPERTS):
        select = (slot == place[:, e : e + 1]).astype(F32).astype(BF)
        total = total + dot(select, x_ref[2 * e])
        total = total + dot(select, x_ref[2 * e + 1])
    out_ref[...] = total.astype(BF).reshape(shards, rows, depth)


def sum_kernel(x_ref, out_ref):
    out_ref[...] = jnp.sum(x_ref[...].astype(F32), axis=0)


def final_kernel(x_ref, middle_ref, out_ref):
    out_ref[...] = (middle_ref[...] + jnp.sum(x_ref[...].astype(F32), axis=0)).astype(BF)


def local(
    stream,
    mixer_gain,
    in_weight,
    conv_state,
    conv_weight,
    conv_bias,
    proj_weight,
    step_weight,
    step_bias,
    decay_log,
    skip_gain,
    ssm_state,
    out_weight,
    moe_gain,
    routes,
    route_weight,
    gate_weight,
    up_weight,
    down_weight,
):
    side = lax.axis_index("side")
    groups = lax.axis_size("grp")
    shards = lax.axis_size("shard")
    rows, slice_width = stream.shape
    width = in_weight.shape[2]
    side_rows = shards * rows
    slots = shards * CAP

    high, rest = split_wide(moe_gain)
    mid = (moe_gain - high.astype(F32) - rest.astype(F32)).astype(BF)
    lanes = slice_width // rows
    tail = jnp.concatenate([t.reshape(rows, lanes) for t in (high, rest, mid)], axis=1).astype(F32)
    tail = jnp.pad(tail, ((0, 0), (2, 126 - 3 * lanes)))

    near = spread(stream, "shard")
    far = swap(near)

    (packet,) = on_core(
        project_kernel,
        [((groups, rows, 2 * width + 128), BF)],
        near,
        far,
        mixer_gain[None],
        in_weight.reshape(slice_width, 2 * width),
        tail,
    )
    arrived = exchange(packet, "grp")
    some = (rows // 2, proj_weight.shape[0])
    activated, gate, own, other = on_core(
        conv_kernel,
        [((rows, width), BF), ((rows, width), F32), (some, F32), (some, F32)],
        arrived,
        conv_state.transpose(1, 0, 2),
        conv_weight,
        conv_bias[None],
        proj_weight,
    )
    gains = arrived[:, :, 2 * width + 2 : 2 * width + 2 + 3 * lanes].astype(F32)
    gains = jnp.sum(gains.reshape(groups, rows, 3, lanes), axis=2).reshape(groups, slice_width)
    inverse = 1.0 / gains

    (packet,) = on_core(join_kernel, [((shards,) + some, BF)], own, swap(other))
    (own,) = on_core(sum_kernel, [(some, F32)], exchange(packet, "shard"))
    other = swap(own)
    first = side == 0
    params = jnp.concatenate([jnp.where(first, own, other), jnp.where(first, other, own)])

    low = params[:, :RANK].astype(BF)
    entry = params[:, RANK : RANK + NSTATE]
    readout = params[:, RANK + NSTATE :]
    step = jax.nn.softplus(dot(low, step_weight) + step_bias)
    act_wide = activated.astype(F32)
    decay = jnp.exp(-step[:, None, :] * jnp.exp(decay_log)[None])
    new_state = decay * ssm_state + (step * act_wide)[:, None, :] * entry[:, :, None]
    scanned = jnp.sum(new_state * readout[:, :, None], axis=1) + skip_gain * act_wide
    gated = (scanned * gate).astype(BF)

    all_gated = spread(gated, "grp")
    own, other = on_core(
        mixer_out_kernel,
        [((side_rows, slice_width), F32), ((side_rows, slice_width), BF)],
        all_gated,
        out_weight,
    )
    (packet,) = on_core(add_kernel, [((shards, rows, slice_width), BF)], own, swap(other))
    middle, packet = on_core(
        middle_kernel,
        [((rows, slice_width), F32), ((shards, rows, slice_width), BF)],
        exchange(packet, "shard"),
        stream,
        moe_gain[None],
    )
    dense = exchange(packet, "shard")

    place, mixing, place_t = on_core(
        tables_kernel,
        [((EXPERTS, routes.shape[0]), jnp.int32), ((EXPERTS, routes.shape[0]), F32), ((routes.shape[0], 128), jnp.int32)],
        routes.T,
        route_weight.T,
        routes,
    )
    (packet,) = on_core(dispatch_kernel, [((groups, slots, slice_width), BF)], dense, place)
    near = exchange(packet, "grp")
    far = swap(near)

    work = 2 * slots * D * gate_weight.shape[2]
    (hidden,) = on_core(
        near_hidden_kernel,
        [((slots, gate_weight.shape[2]), BF)],
        near,
        inverse,
        gate_weight,
        up_weight,
        flops=2 * work,
    )
    shape = [((groups, slots, slice_width), BF)]
    (other,) = on_core(
        far_kernel, shape, far, inverse, place, mixing, gate_weight, up_weight, down_weight, flops=3 * work
    )
    (packet,) = on_core(near_down_kernel, shape, hidden, place, mixing, down_weight, swap(other), flops=work)
    back = exchange(packet, "grp")

    (packet,) = on_core(combine_kernel, [((shards, rows, slice_width), BF)], back, place_t)
    (mixed,) = on_core(final_kernel, [((rows, slice_width), BF)], exchange(packet, "shard"), middle)
    return (mixed, new_state)


def solution(mesh):
    placed = (
        P(("side", "shard"), "grp"),
        P("grp"),
        P("grp", None, ("side", "shard")),
        P("grp", None, ("side", "shard")),
        P(None, ("side", "shard")),
        P(("side", "shard")),
        P(None, ("side", "shard")),
        P(None, ("side", "shard")),
        P(("side", "shard")),
        P(None, ("side", "shard")),
        P(("side", "shard")),
        P("grp", None, ("side", "shard")),
        P(("side", "shard"), "grp"),
        P("grp"),
        P(),
        P(),
        P("grp", None, ("side", "shard")),
        P("grp", None, ("side", "shard")),
        P("grp", ("side", "shard"), None),
    )
    return jax.shard_map(
        local,
        mesh=mesh,
        in_specs=placed,
        out_specs=(P(("side", "shard"), "grp"), P("grp", None, ("side", "shard"))),
        check_vma=False,
    )
```

```python
import math

import jax
import jax.numpy as jnp
from jax import lax
from jax.experimental import pallas as pl
from jax.experimental.pallas import tpu as pltpu
from jax.sharding import PartitionSpec as P

D = 4096
NSTATE = 16
RANK = 512
EXPERTS = 8
CAP = 20
REQ_DEV = 32
EPS = 1e-06
BF = jnp.bfloat16
F32 = jnp.float32


def on_core(kernel, outs, *operands, flops=0):
    vmem = pl.BlockSpec(memory_space=pltpu.VMEM)
    moved = sum(o.size * o.dtype.itemsize for o in operands)
    limit = moved + sum(math.prod(s) * jnp.dtype(d).itemsize for s, d in outs) + 3 * 2**20
    return pl.pallas_call(
        kernel,
        out_shape=[jax.ShapeDtypeStruct(s, d) for s, d in outs],
        in_specs=[vmem] * len(operands),
        out_specs=[vmem] * len(outs),
        compiler_params=pltpu.CompilerParams(vmem_limit_bytes=limit),
        cost_estimate=pl.CostEstimate(flops=flops, bytes_accessed=moved, transcendentals=0),
    )(*operands)


def dot(a, b):
    return jnp.dot(a, b, preferred_element_type=F32)


def split_wide(values):
    high = values.astype(BF)
    low = (values - high.astype(F32)).astype(BF)
    return high, low


def swap(block):
    return lax.ppermute(block, "side", [(0, 1), (1, 0)])


def exchange(block, axis):
    return lax.all_to_all(block, axis, 0, 0)


def spread(block, axis):
    count = lax.axis_size(axis)
    return exchange(jnp.broadcast_to(block[None], (count,) + block.shape), axis)


def project_kernel(near_ref, far_ref, gain_ref, w_ref, next_gain_ref, out_ref):
    shards, rows, depth = near_ref.shape
    width = w_ref.shape[1]
    side = lax.axis_index("side")
    row = lax.broadcasted_iota(jnp.int32, (rows, 128), 0)
    lane = lax.broadcasted_iota(jnp.int32, (rows, 128), 1)
    gain = next_gain_ref[...]
    high = gain.astype(BF).astype(F32)
    mid = (gain - high).astype(BF).astype(F32)
    low = gain - high - mid
    tail = jnp.zeros((rows, 128), F32)
    for k, term in enumerate((high, mid, low)):
        for h in range(depth // 128):
            tail = jnp.where(row == 2 + 2 * k + h, term[:, h * 128 : (h + 1) * 128], tail)
    for x_ref, c in ((near_ref, side), (far_ref, 1 - side)):
        wide = x_ref[...].reshape(shards * rows, depth).astype(F32)
        squares = jnp.sum(wide * wide, axis=1, keepdims=True)
        part = dot((wide * gain_ref[...]).astype(BF), w_ref[...])
        for z in range(shards):
            span = slice(z * rows, (z + 1) * rows)
            out_ref[c * shards + z, :, :width] = part[span].astype(BF)
            across = jnp.sum(jnp.where(row == lane, squares[span], F32(0.0)), axis=0, keepdims=True)
            high = across.astype(BF).astype(F32)
            extra = jnp.where(row == 0, high, jnp.where(row == 1, across - high, tail))
            out_ref[c * shards + z, :, width:] = extra.astype(BF)


def conv_kernel(x_ref, state_ref, taps_ref, bias_ref, proj_ref, act_ref, gate_ref, own_ref, other_ref, inverse_ref):
    width = act_ref.shape[1]
    total = jnp.sum(x_ref[...].astype(F32), axis=0)
    rows = act_ref.shape[0]
    across = total[0:1, 2 * width :] + total[1:2, 2 * width :]
    same = lax.broadcasted_iota(jnp.int32, (rows, 128), 0) == lax.broadcasted_iota(jnp.int32, (rows, 128), 1)
    squares = jnp.sum(jnp.where(same, across, F32(0.0)), axis=1, keepdims=True)
    scale = lax.rsqrt(squares / D + EPS)
    for s in range(x_ref.shape[0]):
        extra = x_ref[s, :, 2 * width :].astype(F32)
        for h in range(inverse_ref.shape[1] // 128):
            gain = extra[2 + h : 3 + h] + extra[4 + h : 5 + h] + extra[6 + h : 7 + h]
            inverse_ref[s : s + 1, h * 128 : (h + 1) * 128] = 1.0 / gain
    newest = (total[:, :width] * scale).astype(BF).astype(F32)
    gate = (total[:, width : 2 * width] * scale).astype(BF).astype(F32)
    conv = newest * taps_ref[3:4, :]
    for k in range(3):
        conv = conv + state_ref[k].astype(F32) * taps_ref[k : k + 1, :]
    activated = jax.nn.silu(conv + bias_ref[...]).astype(BF)
    act_ref[...] = activated
    gate_ref[...] = jax.nn.silu(gate)
    part = lax.dot_general(
        activated, proj_ref[...], (((1,), (1,)), ((), ())), preferred_element_type=F32
    )
    half = part.shape[0] // 2
    first = lax.axis_index("side") == 0
    own_ref[...] = jnp.where(first, part[:half], part[half:])
    other_ref[...] = jnp.where(first, part[half:], part[:half])


def step_kernel(own_ref, other_ref, act_ref, w_ref, bias_ref, step_ref, driven_ref, entry_ref, readout_ref):
    first = lax.axis_index("side") == 0
    own, other = own_ref[...], other_ref[...]
    params = jnp.concatenate([jnp.where(first, own, other), jnp.where(first, other, own)], axis=0)
    raw = dot(params[:, :RANK].astype(BF), w_ref[...]) + bias_ref[...]
    step = jnp.maximum(raw, 0.0) + jnp.log1p(jnp.exp(-jnp.abs(raw)))
    step_ref[...] = step
    driven_ref[...] = step * act_ref[...].astype(F32)
    entry_ref[...] = params[:, RANK : RANK + NSTATE]
    readout_ref[...] = params[:, RANK + NSTATE :]


def join_kernel(a_ref, b_ref, out_ref):
    joined = (a_ref[...] + b_ref[...]).astype(BF)
    for z in range(out_ref.shape[0]):
        out_ref[z] = joined


def mixer_out_kernel(x_ref, w_ref, own_ref, other_ref):
    groups, rows, width = x_ref.shape
    half = groups // 2
    side = lax.axis_index("side")
    other = x_ref[pl.ds((1 - side) * half, half)].reshape(half * rows, width)
    other_ref[...] = dot(other, w_ref[...]).astype(BF)
    own = x_ref[pl.ds(side * half, half)].reshape(half * rows, width)
    own_ref[...] = dot(own, w_ref[...])


def add_kernel(a_ref, b_ref, out_ref):
    joined = a_ref[...] + b_ref[...].astype(F32)
    out_ref[...] = joined.astype(BF).reshape(out_ref.shape)


def middle_kernel(x_ref, stream_ref, gain_ref, middle_ref, out_ref):
    middle = stream_ref[...].astype(F32) + jnp.sum(x_ref[...].astype(F32), axis=0)
    middle_ref[...] = middle
    scaled = (middle * gain_ref[...]).astype(BF)
    for z in range(out_ref.shape[0]):
        out_ref[z] = scaled


def tables_kernel(routes_ref, weights_ref, place_ref, mixing_ref, place_t_ref):
    requests = routes_ref.shape[1]
    block = REQ_DEV
    half = requests // 2
    early = lax.broadcasted_iota(jnp.int32, (requests, requests), 0)
    late = lax.broadcasted_iota(jnp.int32, (requests, requests), 1)
    upto = ((early // block == late // block) & (early <= late)).astype(F32).astype(BF)

    expert = lax.broadcasted_iota(jnp.int32, (EXPERTS, requests), 0)
    one = routes_ref[0:1, :] == expert
    two = routes_ref[1:2, :] == expert
    mixing_ref[...] = jnp.where(one, weights_ref[0:1, :], F32(0.0)) + jnp.where(two, weights_ref[1:2, :], F32(0.0))
    hits = (one | two).astype(F32)
    slot = dot(hits.astype(BF), upto).astype(jnp.int32) - 1
    request = lax.broadcasted_iota(jnp.int32, (EXPERTS, requests), 1)
    place = jnp.where(one | two, slot + (request % half) // block * CAP, -1)
    place_ref[...] = place
    wide = jnp.concatenate([place, jnp.zeros((128 - EXPERTS, requests), jnp.int32)], axis=0)
    place_t_ref[...] = wide.T


def dispatch_kernel(x_ref, place_ref, out_ref):
    shards, rows, depth = x_ref.shape
    slots = out_ref.shape[1]
    dense = x_ref[...].reshape(shards * rows, depth)
    place = jnp.where(lax.axis_index("side") == 0, place_ref[:, : shards * rows], place_ref[:, shards * rows :])
    slot = lax.broadcasted_iota(jnp.int32, (slots, shards * rows), 0)
    for e in range(EXPERTS):
        select = (slot == place[e : e + 1, :]).astype(F32).astype(BF)
        picked = dot(select, dense).astype(BF)
        out_ref[2 * e] = picked
        out_ref[2 * e + 1] = picked


def expert_hidden(x_ref, inverse_ref, g_ref, u_ref):
    groups, slots, depth = x_ref.shape
    gate = jnp.zeros((slots, g_ref.shape[2]), F32)
    upper = jnp.zeros((slots, g_ref.shape[2]), F32)
    squares = jnp.zeros((slots, 1), F32)
    for s in range(groups):
        span = slice(s * depth, (s + 1) * depth)
        block = x_ref[s]
        gate = gate + dot(block, g_ref[0, span, :])
        upper = upper + dot(block, u_ref[0, span, :])
        plain = block.astype(F32) * inverse_ref[s : s + 1, :]
        squares = squares + jnp.sum(plain * plain, axis=1, keepdims=True)
    scale = lax.rsqrt(squares / D + EPS)
    return (jax.nn.silu(gate * scale) * (upper * scale)).astype(BF)


def slot_weight(slots, place_ref, mixing_ref, far):
    half = place_ref.shape[1] // 2
    expert = lax.axis_index("grp") // 2
    low_half = (lax.axis_index("side") == 0) != far
    row = lax.broadcasted_iota(jnp.int32, place_ref.shape, 0) == expert
    place = jnp.sum(jnp.where(row, place_ref[...], 0), axis=0, keepdims=True)
    mixing = jnp.sum(jnp.where(row, mixing_ref[...], F32(0.0)), axis=0, keepdims=True)
    place = jnp.where(low_half, place[:, :half], place[:, half:])
    mixing = jnp.where(low_half, mixing[:, :half], mixing[:, half:])
    slot = lax.broadcasted_iota(jnp.int32, (slots, half), 0)
    return jnp.sum(jnp.where(slot == place, mixing, F32(0.0)), axis=1, keepdims=True)


def near_hidden_kernel(x_ref, inverse_ref, g_ref, u_ref, out_ref):
    out_ref[...] = expert_hidden(x_ref, inverse_ref, g_ref, u_ref)


def far_kernel(x_ref, inverse_ref, place_ref, mixing_ref, g_ref, u_ref, d_ref, out_ref):
    groups, slots, depth = out_ref.shape
    weight = slot_weight(slots, place_ref, mixing_ref, True)
    hidden = expert_hidden(x_ref, inverse_ref, g_ref, u_ref)
    for s in range(groups):
        out_ref[s] = (dot(hidden, d_ref[0, :, s * depth : (s + 1) * depth]) * weight).astype(BF)


def near_down_kernel(hidden_ref, place_ref, mixing_ref, d_ref, out_ref):
    groups, slots, depth = out_ref.shape
    hidden = hidden_ref[...]
    weight = slot_weight(slots, place_ref, mixing_ref, False)
    for s in range(groups):
        out_ref[s] = dot(hidden, d_ref[0, :, s * depth : (s + 1) * depth]) * weight


def combine_kernel(x_ref, place_ref, out_ref):
    shards, rows, depth = out_ref.shape
    slots = x_ref.shape[1]
    half = shards * rows
    place = jnp.where(lax.axis_index("side") == 0, place_ref[:half, :], place_ref[half:, :])
    slot = lax.broadcasted_iota(jnp.int32, (half, slots), 1)
    total = jnp.zeros((half, depth), F32)
    for e in range(EXPERTS):
        select = (slot == place[:, e : e + 1]).astype(F32).astype(BF)
        total = total + dot(select, x_ref[2 * e])
        total = total + dot(select, x_ref[2 * e + 1])
    out_ref[...] = total.astype(BF).reshape(shards, rows, depth)


def sum_kernel(x_ref, out_ref):
    out_ref[...] = jnp.sum(x_ref[...].astype(F32), axis=0)


def final_kernel(x_ref, middle_ref, out_ref):
    out_ref[...] = (middle_ref[...] + jnp.sum(x_ref[...].astype(F32), axis=0)).astype(BF)


def local(
    stream,
    mixer_gain,
    in_weight,
    conv_state,
    conv_weight,
    conv_bias,
    proj_weight,
    step_weight,
    step_bias,
    decay_log,
    skip_gain,
    ssm_state,
    out_weight,
    moe_gain,
    routes,
    route_weight,
    gate_weight,
    up_weight,
    down_weight,
):
    groups = lax.axis_size("grp")
    shards = lax.axis_size("shard")
    rows, slice_width = stream.shape
    width = in_weight.shape[2]
    side_rows = shards * rows
    slots = shards * CAP

    near = spread(stream, "shard")
    far = swap(near)

    (packet,) = on_core(
        project_kernel,
        [((groups, rows, 2 * width + 128), BF)],
        near,
        far,
        mixer_gain[None],
        in_weight.reshape(slice_width, 2 * width),
        moe_gain[None],
    )
    arrived = exchange(packet, "grp")
    some = (rows // 2, proj_weight.shape[0])
    activated, gate, own, other, inverse = on_core(
        conv_kernel,
        [((rows, width), BF), ((rows, width), F32), (some, F32), (some, F32), ((groups, slice_width), F32)],
        arrived,
        conv_state.transpose(1, 0, 2),
        conv_weight,
        conv_bias[None],
        proj_weight,
    )

    listed, listed_weight, own = lax.optimization_barrier((routes.T, route_weight.T, own))
    requests = routes.shape[0]
    place, mixing, place_t = on_core(
        tables_kernel,
        [((EXPERTS, requests), jnp.int32), ((EXPERTS, requests), F32), ((requests, 128), jnp.int32)],
        listed,
        listed_weight,
    )
    own, place, mixing, place_t = lax.optimization_barrier((own, place, mixing, place_t))

    (packet,) = on_core(join_kernel, [((shards,) + some, BF)], own, swap(other))
    (own,) = on_core(sum_kernel, [(some, F32)], exchange(packet, "shard"))
    step, driven, entry, readout = on_core(
        step_kernel,
        [((rows, width), F32), ((rows, width), F32), ((rows, NSTATE), F32), ((rows, NSTATE), F32)],
        own,
        swap(own),
        activated,
        step_weight,
        step_bias[None],
    )
    act_wide = activated.astype(F32)
    decay = jnp.exp(-step[:, None, :] * jnp.exp(decay_log)[None])
    new_state = decay * ssm_state + driven[:, None, :] * entry[:, :, None]
    scanned = jnp.sum(new_state * readout[:, :, None], axis=1) + skip_gain * act_wide
    gated = (scanned * gate).astype(BF)

    all_gated = spread(gated, "grp")
    own, other = on_core(
        mixer_out_kernel,
        [((side_rows, slice_width), F32), ((side_rows, slice_width), BF)],
        all_gated,
        out_weight,
    )
    (packet,) = on_core(add_kernel, [((shards, rows, slice_width), BF)], own, swap(other))
    middle, packet = on_core(
        middle_kernel,
        [((rows, slice_width), F32), ((shards, rows, slice_width), BF)],
        exchange(packet, "shard"),
        stream,
        moe_gain[None],
    )
    dense = exchange(packet, "shard")

    (packet,) = on_core(dispatch_kernel, [((groups, slots, slice_width), BF)], dense, place)
    near = exchange(packet, "grp")
    far = swap(near)

    work = 2 * slots * D * gate_weight.shape[2]
    (hidden,) = on_core(
        near_hidden_kernel,
        [((slots, gate_weight.shape[2]), BF)],
        near,
        inverse,
        gate_weight,
        up_weight,
        flops=2 * work,
    )
    far, hidden = lax.optimization_barrier((far, hidden))
    shape = (groups, slots, slice_width)
    (other,) = on_core(
        far_kernel,
        [(shape, BF)],
        far,
        inverse,
        place,
        mixing,
        gate_weight,
        up_weight,
        down_weight,
        flops=3 * work,
    )
    (own,) = on_core(near_down_kernel, [(shape, F32)], hidden, place, mixing, down_weight, flops=work)
    other, own = lax.optimization_barrier((swap(other), own))
    (packet,) = on_core(add_kernel, [(shape, BF)], own, other)
    back = exchange(packet, "grp")

    (packet,) = on_core(combine_kernel, [((shards, rows, slice_width), BF)], back, place_t)
    (mixed,) = on_core(final_kernel, [((rows, slice_width), BF)], exchange(packet, "shard"), middle)
    return (mixed, new_state)


def solution(mesh):
    placed = (
        P(("side", "shard"), "grp"),
        P("grp"),
        P("grp", None, ("side", "shard")),
        P("grp", None, ("side", "shard")),
        P(None, ("side", "shard")),
        P(("side", "shard")),
        P(None, ("side", "shard")),
        P(None, ("side", "shard")),
        P(("side", "shard")),
        P(None, ("side", "shard")),
        P(("side", "shard")),
        P("grp", None, ("side", "shard")),
        P(("side", "shard"), "grp"),
        P("grp"),
        P(),
        P(),
        P("grp", None, ("side", "shard")),
        P("grp", None, ("side", "shard")),
        P("grp", ("side", "shard"), None),
    )
    return jax.shard_map(
        local,
        mesh=mesh,
        in_specs=placed,
        out_specs=(P(("side", "shard"), "grp"), P("grp", None, ("side", "shard"))),
        check_vma=False,
    )
```

```python
import math

import jax
import jax.numpy as jnp
from jax import lax
from jax.experimental import pallas as pl
from jax.experimental.pallas import tpu as pltpu
from jax.sharding import PartitionSpec as P

D = 4096
NSTATE = 16
RANK = 512
EXPERTS = 8
CAP = 20
REQ_DEV = 32
EPS = 1e-06
BF = jnp.bfloat16
F32 = jnp.float32


def on_core(kernel, outs, *operands, scratch=(), flops=0):
    vmem = pl.BlockSpec(memory_space=pltpu.VMEM)
    moved = sum(o.size * o.dtype.itemsize for o in operands)
    limit = moved + sum(math.prod(s) * jnp.dtype(d).itemsize for s, d in outs) + 3 * 2**20
    return pl.pallas_call(
        kernel,
        out_shape=[jax.ShapeDtypeStruct(s, d) for s, d in outs],
        in_specs=[vmem] * len(operands),
        out_specs=[vmem] * len(outs),
        scratch_shapes=scratch,
        compiler_params=pltpu.CompilerParams(vmem_limit_bytes=limit),
        cost_estimate=pl.CostEstimate(flops=flops, bytes_accessed=moved, transcendentals=0),
    )(*operands)


def dot(a, b):
    return jnp.dot(a, b, preferred_element_type=F32)


def split_wide(values):
    high = values.astype(BF)
    low = (values - high.astype(F32)).astype(BF)
    return high, low


def swap(block):
    return lax.ppermute(block, "side", [(0, 1), (1, 0)])


def exchange(block, axis):
    return lax.all_to_all(block, axis, 0, 0)


def spread(block, axis):
    count = lax.axis_size(axis)
    return exchange(jnp.broadcast_to(block[None], (count,) + block.shape), axis)


def project_kernel(near_ref, far_ref, gain_ref, w_ref, next_gain_ref, out_ref):
    shards, rows, depth = near_ref.shape
    tiles = w_ref.shape[1] // 128
    side = lax.axis_index("side")
    same = lax.broadcasted_iota(jnp.int32, (rows, 128), 0) == lax.broadcasted_iota(jnp.int32, (rows, 128), 1)
    row = lax.broadcasted_iota(jnp.int32, (16, 128), 0)
    gain = next_gain_ref[...]
    high = gain.astype(BF).astype(F32)
    mid = (gain - high).astype(BF).astype(F32)
    low = gain - high - mid
    tail = jnp.zeros((16, 128), F32)
    for k, term in enumerate((high, mid, low)):
        for h in range(depth // 128):
            tail = jnp.where(row == 2 + 2 * k + h, term[:, h * 128 : (h + 1) * 128], tail)
    for block_ref, c in ((near_ref, side), (far_ref, 1 - side)):
        wide = block_ref[...].reshape(shards * rows, depth).astype(F32)
        squares = jnp.sum(wide * wide, axis=1, keepdims=True)
        part = dot((wide * gain_ref[...]).astype(BF), w_ref[...])
        for z in range(shards):
            span = slice(z * rows, (z + 1) * rows)
            for t in range(tiles):
                out_ref[c * shards + z, t * rows : (t + 1) * rows, :] = part[span, t * 128 : (t + 1) * 128].astype(BF)
            across = jnp.sum(jnp.where(same, squares[span], F32(0.0)), axis=0, keepdims=True)
            high = across.astype(BF).astype(F32)
            extra = jnp.where(row == 0, high, jnp.where(row == 1, across - high, tail))
            out_ref[c * shards + z, tiles * rows :, :] = extra.astype(BF)


def conv_kernel(
    x_ref, state_ref, taps_ref, bias_ref, proj_ref, act_ref, gate_ref, own_ref, other_ref, inverse_ref
):
    rows, width = act_ref.shape
    tiles = width // 128
    total = jnp.sum(x_ref[...].astype(F32), axis=0)
    end = 2 * tiles * rows
    across = total[end : end + 1] + total[end + 1 : end + 2]
    same = lax.broadcasted_iota(jnp.int32, (rows, 128), 0) == lax.broadcasted_iota(jnp.int32, (rows, 128), 1)
    squares = jnp.sum(jnp.where(same, across, F32(0.0)), axis=1, keepdims=True)
    scale = lax.rsqrt(squares / D + EPS)
    for s in range(x_ref.shape[0]):
        extra = x_ref[s, end:, :].astype(F32)
        for h in range(inverse_ref.shape[1] // 128):
            gain = extra[2 + h : 3 + h] + extra[4 + h : 5 + h] + extra[6 + h : 7 + h]
            inverse_ref[s : s + 1, h * 128 : (h + 1) * 128] = 1.0 / gain
    columns = [total[t * rows : (t + 1) * rows] for t in range(2 * tiles)]
    newest = (jnp.concatenate(columns[:tiles], axis=1) * scale).astype(BF).astype(F32)
    gate = (jnp.concatenate(columns[tiles:], axis=1) * scale).astype(BF).astype(F32)
    gate_ref[...] = jax.nn.silu(gate)
    conv = newest * taps_ref[3:4, :]
    for k in range(3):
        conv = conv + state_ref[k].astype(F32) * taps_ref[k : k + 1, :]
    activated = jax.nn.silu(conv + bias_ref[...]).astype(BF)
    act_ref[...] = activated
    part = lax.dot_general(
        activated, proj_ref[...], (((1,), (1,)), ((), ())), preferred_element_type=F32
    )
    half = part.shape[0] // 2
    first = lax.axis_index("side") == 0
    own_ref[...] = jnp.where(first, part[:half], part[half:])
    other_ref[...] = jnp.where(first, part[half:], part[:half])


def state_kernel(
    own_ref, other_ref, act_ref, gate_ref, w_ref, bias_ref, decay_ref, skip_ref, old_ref, new_ref, out_ref, step_ref, scan_ref
):
    rows, width = act_ref.shape
    first = lax.axis_index("side") == 0
    own, other = own_ref[...], other_ref[...]
    params = jnp.concatenate([jnp.where(first, own, other), jnp.where(first, other, own)], axis=0)
    raw = dot(params[:, :RANK].astype(BF), w_ref[...]) + bias_ref[...]
    step_ref[...] = jnp.maximum(raw, 0.0) + jnp.log1p(jnp.exp(-jnp.abs(raw)))
    act = act_ref[...].astype(F32)
    ends = jnp.concatenate([params[:, RANK:], jnp.zeros((rows, 128 - 2 * NSTATE), F32)], axis=1).T
    rate = -jnp.exp(decay_ref[...])
    for r in range(rows):
        step = step_ref[r : r + 1, :]
        entry = ends[:NSTATE, r : r + 1]
        readout = ends[NSTATE : 2 * NSTATE, r : r + 1]
        state = jnp.exp(step * rate) * old_ref[r] + (step * act[r : r + 1, :]) * entry
        new_ref[r] = state
        scan_ref[r : r + 1, :] = jnp.sum(state * readout, axis=0, keepdims=True)
    gated = ((scan_ref[...] + skip_ref[...] * act) * gate_ref[...]).astype(BF)
    for s in range(out_ref.shape[0]):
        out_ref[s] = gated


def join_kernel(a_ref, b_ref, out_ref):
    joined = (a_ref[...] + b_ref[...]).astype(BF)
    for z in range(out_ref.shape[0]):
        out_ref[z] = joined


def mixer_out_kernel(x_ref, w_ref, own_ref, other_ref):
    groups, rows, width = x_ref.shape
    half = groups // 2
    side = lax.axis_index("side")
    other = x_ref[pl.ds((1 - side) * half, half)].reshape(half * rows, width)
    other_ref[...] = dot(other, w_ref[...]).astype(BF)
    own = x_ref[pl.ds(side * half, half)].reshape(half * rows, width)
    own_ref[...] = dot(own, w_ref[...])


def add_kernel(a_ref, b_ref, out_ref):
    joined = a_ref[...] + b_ref[...].astype(F32)
    out_ref[...] = joined.astype(BF).reshape(out_ref.shape)


def middle_kernel(x_ref, stream_ref, gain_ref, middle_ref, out_ref):
    middle = stream_ref[...].astype(F32) + jnp.sum(x_ref[...].astype(F32), axis=0)
    middle_ref[...] = middle
    scaled = (middle * gain_ref[...]).astype(BF)
    for z in range(out_ref.shape[0]):
        out_ref[z] = scaled


def tables_kernel(routes_ref, weights_ref, place_ref, mixing_ref, place_t_ref):
    requests = routes_ref.shape[1]
    block = REQ_DEV
    half = requests // 2
    early = lax.broadcasted_iota(jnp.int32, (requests, requests), 0)
    late = lax.broadcasted_iota(jnp.int32, (requests, requests), 1)
    upto = ((early // block == late // block) & (early <= late)).astype(F32).astype(BF)

    expert = lax.broadcasted_iota(jnp.int32, (EXPERTS, requests), 0)
    one = routes_ref[0:1, :] == expert
    two = routes_ref[1:2, :] == expert
    mixing_ref[...] = jnp.where(one, weights_ref[0:1, :], F32(0.0)) + jnp.where(two, weights_ref[1:2, :], F32(0.0))
    hits = (one | two).astype(F32)
    slot = dot(hits.astype(BF), upto).astype(jnp.int32) - 1
    request = lax.broadcasted_iota(jnp.int32, (EXPERTS, requests), 1)
    place = jnp.where(one | two, slot + (request % half) // block * CAP, -1)
    place_ref[...] = place
    wide = jnp.concatenate([place, jnp.zeros((128 - EXPERTS, requests), jnp.int32)], axis=0)
    place_t_ref[...] = wide.T


def dispatch_kernel(x_ref, place_ref, out_ref):
    shards, rows, depth = x_ref.shape
    slots = out_ref.shape[1]
    dense = x_ref[...].reshape(shards * rows, depth)
    place = jnp.where(lax.axis_index("side") == 0, place_ref[:, : shards * rows], place_ref[:, shards * rows :])
    slot = lax.broadcasted_iota(jnp.int32, (slots, shards * rows), 0)
    for e in range(EXPERTS):
        select = (slot == place[e : e + 1, :]).astype(F32).astype(BF)
        picked = dot(select, dense).astype(BF)
        out_ref[2 * e] = picked
        out_ref[2 * e + 1] = picked


def expert_hidden(x_ref, inverse_ref, g_ref, u_ref):
    groups, slots, depth = x_ref.shape
    gate = jnp.zeros((slots, g_ref.shape[2]), F32)
    upper = jnp.zeros((slots, g_ref.shape[2]), F32)
    squares = jnp.zeros((slots, 1), F32)
    for s in range(groups):
        span = slice(s * depth, (s + 1) * depth)
        block = x_ref[s]
        gate = gate + dot(block, g_ref[0, span, :])
        upper = upper + dot(block, u_ref[0, span, :])
        plain = block.astype(F32) * inverse_ref[s : s + 1, :]
        squares = squares + jnp.sum(plain * plain, axis=1, keepdims=True)
    scale = lax.rsqrt(squares / D + EPS)
    return (jax.nn.silu(gate * scale) * (upper * scale)).astype(BF)


def slot_weight(slots, place_ref, mixing_ref, far):
    half = place_ref.shape[1] // 2
    expert = lax.axis_index("grp") // 2
    low_half = (lax.axis_index("side") == 0) != far
    row = lax.broadcasted_iota(jnp.int32, place_ref.shape, 0) == expert
    place = jnp.sum(jnp.where(row, place_ref[...], 0), axis=0, keepdims=True)
    mixing = jnp.sum(jnp.where(row, mixing_ref[...], F32(0.0)), axis=0, keepdims=True)
    place = jnp.where(low_half, place[:, :half], place[:, half:])
    mixing = jnp.where(low_half, mixing[:, :half], mixing[:, half:])
    slot = lax.broadcasted_iota(jnp.int32, (slots, half), 0)
    return jnp.sum(jnp.where(slot == place, mixing, F32(0.0)), axis=1, keepdims=True)


def near_hidden_kernel(x_ref, inverse_ref, g_ref, u_ref, out_ref):
    out_ref[...] = expert_hidden(x_ref, inverse_ref, g_ref, u_ref)


def far_kernel(x_ref, inverse_ref, place_ref, mixing_ref, g_ref, u_ref, d_ref, out_ref):
    groups, slots, depth = out_ref.shape
    weight = slot_weight(slots, place_ref, mixing_ref, True)
    hidden = expert_hidden(x_ref, inverse_ref, g_ref, u_ref)
    for s in range(groups):
        out_ref[s] = (dot(hidden, d_ref[0, :, s * depth : (s + 1) * depth]) * weight).astype(BF)


def near_down_kernel(hidden_ref, place_ref, mixing_ref, d_ref, out_ref):
    groups, slots, depth = out_ref.shape
    hidden = hidden_ref[...]
    weight = slot_weight(slots, place_ref, mixing_ref, False)
    for s in range(groups):
        out_ref[s] = dot(hidden, d_ref[0, :, s * depth : (s + 1) * depth]) * weight


def combine_kernel(x_ref, place_ref, out_ref):
    shards, rows, depth = out_ref.shape
    slots = x_ref.shape[1]
    half = shards * rows
    place = jnp.where(lax.axis_index("side") == 0, place_ref[:half, :], place_ref[half:, :])
    slot = lax.broadcasted_iota(jnp.int32, (half, slots), 1)
    total = jnp.zeros((half, depth), F32)
    for e in range(EXPERTS):
        select = (slot == place[:, e : e + 1]).astype(F32).astype(BF)
        total = total + dot(select, x_ref[2 * e])
        total = total + dot(select, x_ref[2 * e + 1])
    out_ref[...] = total.astype(BF).reshape(shards, rows, depth)


def sum_kernel(x_ref, out_ref):
    out_ref[...] = jnp.sum(x_ref[...].astype(F32), axis=0)


def final_kernel(x_ref, middle_ref, out_ref):
    out_ref[...] = (middle_ref[...] + jnp.sum(x_ref[...].astype(F32), axis=0)).astype(BF)


def local(
    stream,
    mixer_gain,
    in_weight,
    conv_state,
    conv_weight,
    conv_bias,
    proj_weight,
    step_weight,
    step_bias,
    decay_log,
    skip_gain,
    ssm_state,
    out_weight,
    moe_gain,
    routes,
    route_weight,
    gate_weight,
    up_weight,
    down_weight,
):
    groups = lax.axis_size("grp")
    shards = lax.axis_size("shard")
    rows, slice_width = stream.shape
    width = in_weight.shape[2]
    side_rows = shards * rows
    slots = shards * CAP

    near = spread(stream, "shard")
    far = swap(near)

    (packet,) = on_core(
        project_kernel,
        [((groups, 2 * width // 128 * rows + 16, 128), BF)],
        near,
        far,
        mixer_gain[None],
        in_weight.reshape(slice_width, 2 * width),
        moe_gain[None],
    )
    arrived = exchange(packet, "grp")
    some = (rows // 2, proj_weight.shape[0])
    activated, gate, own, other, inverse = on_core(
        conv_kernel,
        [((rows, width), BF), ((rows, width), F32), (some, F32), (some, F32), ((groups, slice_width), F32)],
        arrived,
        conv_state.transpose(1, 0, 2),
        conv_weight,
        conv_bias[None],
        proj_weight,
    )

    listed, listed_weight, own = lax.optimization_barrier((routes.T, route_weight.T, own))
    requests = routes.shape[0]
    place, mixing, place_t = on_core(
        tables_kernel,
        [((EXPERTS, requests), jnp.int32), ((EXPERTS, requests), F32), ((requests, 128), jnp.int32)],
        listed,
        listed_weight,
    )
    own, place, mixing, place_t = lax.optimization_barrier((own, place, mixing, place_t))

    (packet,) = on_core(join_kernel, [((shards,) + some, BF)], own, swap(other))
    (own,) = on_core(sum_kernel, [(some, F32)], exchange(packet, "shard"))
    new_state, packet = on_core(
        state_kernel,
        [(ssm_state.shape, F32), ((groups, rows, width), BF)],
        own,
        swap(own),
        activated,
        gate,
        step_weight,
        step_bias[None],
        decay_log,
        skip_gain[None],
        ssm_state,
        scratch=[pltpu.VMEM((rows, width), F32)] * 2,
    )

    all_gated = exchange(packet, "grp")
    own, other = on_core(
        mixer_out_kernel,
        [((side_rows, slice_width), F32), ((side_rows, slice_width), BF)],
        all_gated,
        out_weight,
    )
    (packet,) = on_core(add_kernel, [((shards, rows, slice_width), BF)], own, swap(other))
    middle, packet = on_core(
        middle_kernel,
        [((rows, slice_width), F32), ((shards, rows, slice_width), BF)],
        exchange(packet, "shard"),
        stream,
        moe_gain[None],
    )
    dense = exchange(packet, "shard")

    (packet,) = on_core(dispatch_kernel, [((groups, slots, slice_width), BF)], dense, place)
    near = exchange(packet, "grp")
    far = swap(near)

    work = 2 * slots * D * gate_weight.shape[2]
    (hidden,) = on_core(
        near_hidden_kernel,
        [((slots, gate_weight.shape[2]), BF)],
        near,
        inverse,
        gate_weight,
        up_weight,
        flops=2 * work,
    )
    far, hidden = lax.optimization_barrier((far, hidden))
    shape = (groups, slots, slice_width)
    (other,) = on_core(
        far_kernel,
        [(shape, BF)],
        far,
        inverse,
        place,
        mixing,
        gate_weight,
        up_weight,
        down_weight,
        flops=3 * work,
    )
    (own,) = on_core(near_down_kernel, [(shape, F32)], hidden, place, mixing, down_weight, flops=work)
    other, own = lax.optimization_barrier((swap(other), own))
    (packet,) = on_core(add_kernel, [(shape, BF)], own, other)
    back = exchange(packet, "grp")

    (packet,) = on_core(combine_kernel, [((shards, rows, slice_width), BF)], back, place_t)
    (mixed,) = on_core(final_kernel, [((rows, slice_width), BF)], exchange(packet, "shard"), middle)
    return (mixed, new_state)


def solution(mesh):
    placed = (
        P(("side", "shard"), "grp"),
        P("grp"),
        P("grp", None, ("side", "shard")),
        P("grp", None, ("side", "shard")),
        P(None, ("side", "shard")),
        P(("side", "shard")),
        P(None, ("side", "shard")),
        P(None, ("side", "shard")),
        P(("side", "shard")),
        P(None, ("side", "shard")),
        P(("side", "shard")),
        P("grp", None, ("side", "shard")),
        P(("side", "shard"), "grp"),
        P("grp"),
        P(),
        P(),
        P("grp", None, ("side", "shard")),
        P("grp", None, ("side", "shard")),
        P("grp", ("side", "shard"), None),
    )
    return jax.shard_map(
        local,
        mesh=mesh,
        in_specs=placed,
        out_specs=(P(("side", "shard"), "grp"), P("grp", None, ("side", "shard"))),
        check_vma=False,
    )
```

```python
import math

import jax
import jax.numpy as jnp
from jax import lax
from jax.experimental import pallas as pl
from jax.experimental.pallas import tpu as pltpu
from jax.sharding import PartitionSpec as P

D = 4096
NSTATE = 16
RANK = 512
EXPERTS = 8
CAP = 20
REQ_DEV = 32
EPS = 1e-06
BF = jnp.bfloat16
F32 = jnp.float32


def on_core(kernel, outs, *operands, scratch=(), flops=0, limit=0):
    vmem = pl.BlockSpec(memory_space=pltpu.VMEM)
    moved = sum(o.size * o.dtype.itemsize for o in operands)
    limit = limit or moved + sum(math.prod(s) * jnp.dtype(d).itemsize for s, d in outs) + 3 * 2**20
    return pl.pallas_call(
        kernel,
        out_shape=[jax.ShapeDtypeStruct(s, d) for s, d in outs],
        in_specs=[vmem] * len(operands),
        out_specs=[vmem] * len(outs),
        scratch_shapes=scratch,
        compiler_params=pltpu.CompilerParams(vmem_limit_bytes=limit),
        cost_estimate=pl.CostEstimate(flops=flops, bytes_accessed=moved, transcendentals=0),
    )(*operands)


def dot(a, b):
    return jnp.dot(a, b, preferred_element_type=F32)


def split_wide(values):
    high = values.astype(BF)
    low = (values - high.astype(F32)).astype(BF)
    return high, low


def swap(block):
    return lax.ppermute(block, "side", [(0, 1), (1, 0)])


def exchange(block, axis):
    return lax.all_to_all(block, axis, 0, 0)


def spread(block, axis):
    count = lax.axis_size(axis)
    return exchange(jnp.broadcast_to(block[None], (count,) + block.shape), axis)


def project_kernel(near_ref, far_ref, gains_ref, w_ref, out_ref):
    shards, rows, depth = near_ref.shape
    tiles = w_ref.shape[1] // 128
    side = lax.axis_index("side")
    same = lax.broadcasted_iota(jnp.int32, (rows, 128), 0) == lax.broadcasted_iota(jnp.int32, (rows, 128), 1)
    row = lax.broadcasted_iota(jnp.int32, (16, 128), 0)
    gain = gains_ref[1:2, :]
    high = gain.astype(BF).astype(F32)
    mid = (gain - high).astype(BF).astype(F32)
    low = gain - high - mid
    tail = jnp.zeros((16, 128), F32)
    for k, term in enumerate((high, mid, low)):
        for h in range(depth // 128):
            tail = jnp.where(row == 2 + 2 * k + h, term[:, h * 128 : (h + 1) * 128], tail)
    for block_ref, c in ((near_ref, side), (far_ref, 1 - side)):
        wide = block_ref[...].reshape(shards * rows, depth).astype(F32)
        squares = jnp.sum(wide * wide, axis=1, keepdims=True)
        part = dot((wide * gains_ref[0:1, :]).astype(BF), w_ref[...])
        for z in range(shards):
            span = slice(z * rows, (z + 1) * rows)
            for t in range(tiles):
                out_ref[c * shards + z, t * rows : (t + 1) * rows, :] = part[span, t * 128 : (t + 1) * 128].astype(BF)
            across = jnp.sum(jnp.where(same, squares[span], F32(0.0)), axis=0, keepdims=True)
            high = across.astype(BF).astype(F32)
            extra = jnp.where(row == 0, high, jnp.where(row == 1, across - high, tail))
            out_ref[c * shards + z, tiles * rows :, :] = extra.astype(BF)


def conv_kernel(
    x_ref, state_ref, taps_ref, bias_ref, proj_ref, act_ref, gate_ref, own_ref, other_ref, inverse_ref
):
    rows, width = act_ref.shape
    tiles = width // 128
    total = jnp.sum(x_ref[...].astype(F32), axis=0)
    end = 2 * tiles * rows
    across = total[end : end + 1] + total[end + 1 : end + 2]
    same = lax.broadcasted_iota(jnp.int32, (rows, 128), 0) == lax.broadcasted_iota(jnp.int32, (rows, 128), 1)
    squares = jnp.sum(jnp.where(same, across, F32(0.0)), axis=1, keepdims=True)
    scale = lax.rsqrt(squares / D + EPS)
    for s in range(x_ref.shape[0]):
        extra = x_ref[s, end:, :].astype(F32)
        for h in range(inverse_ref.shape[1] // 128):
            gain = extra[2 + h : 3 + h] + extra[4 + h : 5 + h] + extra[6 + h : 7 + h]
            inverse_ref[s : s + 1, h * 128 : (h + 1) * 128] = 1.0 / gain
    columns = [total[t * rows : (t + 1) * rows] for t in range(2 * tiles)]
    newest = (jnp.concatenate(columns[:tiles], axis=1) * scale).astype(BF).astype(F32)
    gate = (jnp.concatenate(columns[tiles:], axis=1) * scale).astype(BF).astype(F32)
    gate_ref[...] = jax.nn.silu(gate)
    conv = newest * taps_ref[3:4, :]
    for k in range(3):
        conv = conv + state_ref[k].astype(F32) * taps_ref[k : k + 1, :]
    activated = jax.nn.silu(conv + bias_ref[...]).astype(BF)
    act_ref[...] = activated
    part = lax.dot_general(
        activated, proj_ref[...], (((1,), (1,)), ((), ())), preferred_element_type=F32
    )
    half = part.shape[0] // 2
    first = lax.axis_index("side") == 0
    own_ref[...] = jnp.where(first, part[:half], part[half:])
    other_ref[...] = jnp.where(first, part[half:], part[:half])


def state_kernel(
    own_ref, other_ref, act_ref, gate_ref, w_ref, bias_ref, decay_ref, skip_ref, old_ref, new_ref, out_ref, step_ref, scan_ref
):
    rows, width = act_ref.shape
    first = lax.axis_index("side") == 0
    own, other = own_ref[...], other_ref[...]
    params = jnp.concatenate([jnp.where(first, own, other), jnp.where(first, other, own)], axis=0)
    raw = dot(params[:, :RANK].astype(BF), w_ref[...]) + bias_ref[...]
    step_ref[...] = jnp.maximum(raw, 0.0) + jnp.log1p(jnp.exp(-jnp.abs(raw)))
    act = act_ref[...].astype(F32)
    ends = jnp.concatenate([params[:, RANK:], jnp.zeros((rows, 128 - 2 * NSTATE), F32)], axis=1).T
    rate = -jnp.exp(decay_ref[...])
    for r in range(rows):
        step = step_ref[r : r + 1, :]
        entry = ends[:NSTATE, r : r + 1]
        readout = ends[NSTATE : 2 * NSTATE, r : r + 1]
        state = jnp.exp(step * rate) * old_ref[r] + (step * act[r : r + 1, :]) * entry
        new_ref[r] = state
        scan_ref[r : r + 1, :] = jnp.sum(state * readout, axis=0, keepdims=True)
    gated = ((scan_ref[...] + skip_ref[...] * act) * gate_ref[...]).astype(BF)
    for s in range(out_ref.shape[0]):
        out_ref[s] = gated


def join_kernel(a_ref, b_ref, out_ref):
    joined = (a_ref[...] + b_ref[...]).astype(BF)
    for z in range(out_ref.shape[0]):
        out_ref[z] = joined


def mixer_out_kernel(x_ref, w_ref, own_ref, other_ref):
    groups, rows, width = x_ref.shape
    half = groups // 2
    side = lax.axis_index("side")
    other = x_ref[pl.ds((1 - side) * half, half)].reshape(half * rows, width)
    other_ref[...] = dot(other, w_ref[...]).astype(BF)
    own = x_ref[pl.ds(side * half, half)].reshape(half * rows, width)
    own_ref[...] = dot(own, w_ref[...])


def add_kernel(a_ref, b_ref, out_ref):
    joined = a_ref[...] + b_ref[...].astype(F32)
    out_ref[...] = joined.astype(BF).reshape(out_ref.shape)


def middle_kernel(x_ref, stream_ref, gain_ref, middle_ref, out_ref):
    middle = stream_ref[...].astype(F32) + jnp.sum(x_ref[...].astype(F32), axis=0)
    middle_ref[...] = middle
    scaled = (middle * gain_ref[...]).astype(BF)
    for z in range(out_ref.shape[0]):
        out_ref[z] = scaled


def tables_kernel(routes_ref, weights_ref, place_ref, mixing_ref, place_t_ref):
    requests = routes_ref.shape[1]
    block = REQ_DEV
    half = requests // 2
    early = lax.broadcasted_iota(jnp.int32, (requests, requests), 0)
    late = lax.broadcasted_iota(jnp.int32, (requests, requests), 1)
    upto = ((early // block == late // block) & (early <= late)).astype(F32).astype(BF)

    expert = lax.broadcasted_iota(jnp.int32, (EXPERTS, requests), 0)
    one = routes_ref[0:1, :] == expert
    two = routes_ref[1:2, :] == expert
    mixing_ref[...] = jnp.where(one, weights_ref[0:1, :], F32(0.0)) + jnp.where(two, weights_ref[1:2, :], F32(0.0))
    hits = (one | two).astype(F32)
    slot = dot(hits.astype(BF), upto).astype(jnp.int32) - 1
    request = lax.broadcasted_iota(jnp.int32, (EXPERTS, requests), 1)
    place = jnp.where(one | two, slot + (request % half) // block * CAP, -1)
    place_ref[...] = place
    wide = jnp.concatenate([place, jnp.zeros((128 - EXPERTS, requests), jnp.int32)], axis=0)
    place_t_ref[...] = wide.T


def dispatch_kernel(x_ref, place_ref, out_ref):
    shards, rows, depth = x_ref.shape
    slots = out_ref.shape[1]
    dense = x_ref[...].reshape(shards * rows, depth)
    place = jnp.where(lax.axis_index("side") == 0, place_ref[:, : shards * rows], place_ref[:, shards * rows :])
    slot = lax.broadcasted_iota(jnp.int32, (slots, shards * rows), 0)
    for e in range(EXPERTS):
        select = (slot == place[e : e + 1, :]).astype(F32).astype(BF)
        picked = dot(select, dense).astype(BF)
        out_ref[2 * e] = picked
        out_ref[2 * e + 1] = picked


def hidden_kernel(x_ref, inverse_ref, g_ref, u_ref, out_ref):
    groups, slots, depth = x_ref.shape
    gate = jnp.zeros((slots, g_ref.shape[2]), F32)
    upper = jnp.zeros((slots, g_ref.shape[2]), F32)
    squares = jnp.zeros((slots, 1), F32)
    for s in range(groups):
        span = slice(s * depth, (s + 1) * depth)
        block = x_ref[s]
        gate = gate + dot(block, g_ref[0, span, :])
        upper = upper + dot(block, u_ref[0, span, :])
        plain = block.astype(F32) * inverse_ref[s : s + 1, :]
        squares = squares + jnp.sum(plain * plain, axis=1, keepdims=True)
    scale = lax.rsqrt(squares / D + EPS)
    out_ref[...] = (jax.nn.silu(gate * scale) * (upper * scale)).astype(BF)


def slot_weight(slots, place_ref, mixing_ref):
    half = place_ref.shape[1] // 2
    expert = lax.axis_index("grp") // 2
    first = lax.axis_index("side") == 0
    row = lax.broadcasted_iota(jnp.int32, place_ref.shape, 0) == expert
    place = jnp.sum(jnp.where(row, place_ref[...], 0), axis=0, keepdims=True)
    mixing = jnp.sum(jnp.where(row, mixing_ref[...], F32(0.0)), axis=0, keepdims=True)
    place = jnp.where(first, place[:, :half], place[:, half:])
    mixing = jnp.where(first, mixing[:, :half], mixing[:, half:])
    slot = lax.broadcasted_iota(jnp.int32, (slots, half), 0)
    return jnp.sum(jnp.where(slot == place, mixing, F32(0.0)), axis=1, keepdims=True)


def down_kernel(own_ref, other_ref, place_ref, mixing_ref, own_d_ref, other_d_ref, out_ref):
    groups, slots, depth = out_ref.shape
    own, other = own_ref[...], other_ref[...]
    weight = slot_weight(slots, place_ref, mixing_ref)
    for s in range(groups):
        span = slice(s * depth, (s + 1) * depth)
        part = dot(own, own_d_ref[0, :, span]) + dot(other, other_d_ref[0, :, span])
        out_ref[s] = (part * weight).astype(BF)


def combine_kernel(x_ref, place_ref, out_ref):
    shards, rows, depth = out_ref.shape
    slots = x_ref.shape[1]
    half = shards * rows
    place = jnp.where(lax.axis_index("side") == 0, place_ref[:half, :], place_ref[half:, :])
    slot = lax.broadcasted_iota(jnp.int32, (half, slots), 1)
    total = jnp.zeros((half, depth), F32)
    for e in range(EXPERTS):
        select = (slot == place[:, e : e + 1]).astype(F32).astype(BF)
        total = total + dot(select, x_ref[2 * e])
        total = total + dot(select, x_ref[2 * e + 1])
    out_ref[...] = total.astype(BF).reshape(shards, rows, depth)


def sum_kernel(x_ref, out_ref):
    out_ref[...] = jnp.sum(x_ref[...].astype(F32), axis=0)


def final_kernel(x_ref, middle_ref, out_ref):
    out_ref[...] = (middle_ref[...] + jnp.sum(x_ref[...].astype(F32), axis=0)).astype(BF)


def local(
    stream,
    mixer_gain,
    in_weight,
    conv_state,
    conv_weight,
    conv_bias,
    proj_weight,
    step_weight,
    step_bias,
    decay_log,
    skip_gain,
    ssm_state,
    out_weight,
    moe_gain,
    routes,
    route_weight,
    gate_weight,
    up_weight,
    down_weight,
):
    groups = lax.axis_size("grp")
    shards = lax.axis_size("shard")
    rows, slice_width = stream.shape
    width = in_weight.shape[2]
    side_rows = shards * rows
    slots = shards * CAP

    packet = jnp.broadcast_to(stream[None], (shards, rows, slice_width))
    gains = jnp.stack([mixer_gain, moe_gain])
    packet, *sent = lax.optimization_barrier((packet, gate_weight, up_weight, down_weight))
    other_gate, other_up, other_down = [swap(weight) for weight in sent]
    near = exchange(packet, "shard")
    far = swap(near)

    (packet,) = on_core(
        project_kernel,
        [((groups, 2 * width // 128 * rows + 16, 128), BF)],
        near,
        far,
        gains,
        in_weight.reshape(slice_width, 2 * width),
    )
    arrived = exchange(packet, "grp")
    some = (rows // 2, proj_weight.shape[0])
    activated, gate, own, other, inverse = on_core(
        conv_kernel,
        [((rows, width), BF), ((rows, width), F32), (some, F32), (some, F32), ((groups, slice_width), F32)],
        arrived,
        conv_state.transpose(1, 0, 2),
        conv_weight,
        conv_bias[None],
        proj_weight,
    )

    listed, listed_weight, own = lax.optimization_barrier((routes.T, route_weight.T, own))
    requests = routes.shape[0]
    place, mixing, place_t = on_core(
        tables_kernel,
        [((EXPERTS, requests), jnp.int32), ((EXPERTS, requests), F32), ((requests, 128), jnp.int32)],
        listed,
        listed_weight,
    )
    own, place, mixing, place_t = lax.optimization_barrier((own, place, mixing, place_t))

    (packet,) = on_core(join_kernel, [((shards,) + some, BF)], own, swap(other))
    (own,) = on_core(sum_kernel, [(some, F32)], exchange(packet, "shard"))
    new_state, packet = on_core(
        state_kernel,
        [(ssm_state.shape, F32), ((groups, rows, width), BF)],
        own,
        swap(own),
        activated,
        gate,
        step_weight,
        step_bias[None],
        decay_log,
        skip_gain[None],
        ssm_state,
        scratch=[pltpu.VMEM((rows, width), F32)] * 2,
    )

    all_gated = exchange(packet, "grp")
    own, other = on_core(
        mixer_out_kernel,
        [((side_rows, slice_width), F32), ((side_rows, slice_width), BF)],
        all_gated,
        out_weight,
    )
    (packet,) = on_core(add_kernel, [((shards, rows, slice_width), BF)], own, swap(other))
    middle, packet = on_core(
        middle_kernel,
        [((rows, slice_width), F32), ((shards, rows, slice_width), BF)],
        exchange(packet, "shard"),
        stream,
        moe_gain[None],
    )
    dense = exchange(packet, "shard")

    (packet,) = on_core(dispatch_kernel, [((groups, slots, slice_width), BF)], dense, place)
    packet, other_gate, other_up, other_down = lax.optimization_barrier((packet, other_gate, other_up, other_down))
    arrived = exchange(packet, "grp")

    work = 2 * slots * D * gate_weight.shape[2]
    some = [((slots, gate_weight.shape[2]), BF)]
    (own,) = on_core(hidden_kernel, some, arrived, inverse, gate_weight, up_weight, flops=2 * work)
    (other,) = on_core(hidden_kernel, some, arrived, inverse, other_gate, other_up, flops=2 * work)
    (packet,) = on_core(
        down_kernel,
        [((groups, slots, slice_width), BF)],
        own,
        other,
        place,
        mixing,
        down_weight,
        other_down,
        flops=2 * work,
    )
    back = exchange(packet, "grp")

    (packet,) = on_core(combine_kernel, [((shards, rows, slice_width), BF)], back, place_t)
    (mixed,) = on_core(final_kernel, [((rows, slice_width), BF)], exchange(packet, "shard"), middle)
    return (mixed, new_state)


def solution(mesh):
    placed = (
        P(("side", "shard"), "grp"),
        P("grp"),
        P("grp", None, ("side", "shard")),
        P("grp", None, ("side", "shard")),
        P(None, ("side", "shard")),
        P(("side", "shard")),
        P(None, ("side", "shard")),
        P(None, ("side", "shard")),
        P(("side", "shard")),
        P(None, ("side", "shard")),
        P(("side", "shard")),
        P("grp", None, ("side", "shard")),
        P(("side", "shard"), "grp"),
        P("grp"),
        P(),
        P(),
        P("grp", None, ("side", "shard")),
        P("grp", None, ("side", "shard")),
        P("grp", ("side", "shard"), None),
    )
    return jax.shard_map(
        local,
        mesh=mesh,
        in_specs=placed,
        out_specs=(P(("side", "shard"), "grp"), P("grp", None, ("side", "shard"))),
        check_vma=False,
    )
```

```python
import math

import jax
import jax.numpy as jnp
from jax import lax
from jax.experimental import pallas as pl
from jax.experimental.pallas import tpu as pltpu
from jax.sharding import PartitionSpec as P

D = 4096
NSTATE = 16
RANK = 512
EXPERTS = 8
CAP = 20
REQ_DEV = 32
EPS = 1e-06
BF = jnp.bfloat16
F32 = jnp.float32


def on_core(kernel, outs, *operands, scratch=(), flops=0, limit=0):
    vmem = pl.BlockSpec(memory_space=pltpu.VMEM)
    moved = sum(o.size * o.dtype.itemsize for o in operands)
    limit = limit or moved + sum(math.prod(s) * jnp.dtype(d).itemsize for s, d in outs) + 3 * 2**20
    return pl.pallas_call(
        kernel,
        out_shape=[jax.ShapeDtypeStruct(s, d) for s, d in outs],
        in_specs=[vmem] * len(operands),
        out_specs=[vmem] * len(outs),
        scratch_shapes=scratch,
        compiler_params=pltpu.CompilerParams(vmem_limit_bytes=limit),
        cost_estimate=pl.CostEstimate(flops=flops, bytes_accessed=moved, transcendentals=0),
    )(*operands)


def dot(a, b):
    return jnp.dot(a, b, preferred_element_type=F32)


def split_wide(values):
    high = values.astype(BF)
    low = (values - high.astype(F32)).astype(BF)
    return high, low


def swap(block):
    return lax.ppermute(block, "side", [(0, 1), (1, 0)])


def exchange(block, axis):
    return lax.all_to_all(block, axis, 0, 0)


def spread(block, axis):
    count = lax.axis_size(axis)
    return exchange(jnp.broadcast_to(block[None], (count,) + block.shape), axis)


def project_kernel(near_ref, far_ref, gains_ref, w_ref, out_ref):
    shards, rows, depth = near_ref.shape
    tiles = w_ref.shape[1] // 128
    side = lax.axis_index("side")
    same = lax.broadcasted_iota(jnp.int32, (rows, 128), 0) == lax.broadcasted_iota(jnp.int32, (rows, 128), 1)
    row = lax.broadcasted_iota(jnp.int32, (16, 128), 0)
    gain = gains_ref[1:2, :]
    high = gain.astype(BF).astype(F32)
    mid = (gain - high).astype(BF).astype(F32)
    low = gain - high - mid
    tail = jnp.zeros((16, 128), F32)
    for k, term in enumerate((high, mid, low)):
        for h in range(depth // 128):
            tail = jnp.where(row == 2 + 2 * k + h, term[:, h * 128 : (h + 1) * 128], tail)
    for block_ref, c in ((near_ref, side), (far_ref, 1 - side)):
        wide = block_ref[...].reshape(shards * rows, depth).astype(F32)
        squares = jnp.sum(wide * wide, axis=1, keepdims=True)
        part = dot((wide * gains_ref[0:1, :]).astype(BF), w_ref[...])
        for z in range(shards):
            span = slice(z * rows, (z + 1) * rows)
            for t in range(tiles):
                out_ref[c * shards + z, t * rows : (t + 1) * rows, :] = part[span, t * 128 : (t + 1) * 128].astype(BF)
            across = jnp.sum(jnp.where(same, squares[span], F32(0.0)), axis=0, keepdims=True)
            high = across.astype(BF).astype(F32)
            extra = jnp.where(row == 0, high, jnp.where(row == 1, across - high, tail))
            out_ref[c * shards + z, tiles * rows :, :] = extra.astype(BF)


def conv_kernel(
    x_ref, state_ref, taps_ref, bias_ref, proj_ref, act_ref, gate_ref, own_ref, other_ref, inverse_ref
):
    rows, width = act_ref.shape
    tiles = width // 128
    total = jnp.sum(x_ref[...].astype(F32), axis=0)
    end = 2 * tiles * rows
    across = total[end : end + 1] + total[end + 1 : end + 2]
    same = lax.broadcasted_iota(jnp.int32, (rows, 128), 0) == lax.broadcasted_iota(jnp.int32, (rows, 128), 1)
    squares = jnp.sum(jnp.where(same, across, F32(0.0)), axis=1, keepdims=True)
    scale = lax.rsqrt(squares / D + EPS)
    for s in range(x_ref.shape[0]):
        extra = x_ref[s, end:, :].astype(F32)
        for h in range(inverse_ref.shape[1] // 128):
            gain = extra[2 + h : 3 + h] + extra[4 + h : 5 + h] + extra[6 + h : 7 + h]
            inverse_ref[s : s + 1, h * 128 : (h + 1) * 128] = 1.0 / gain
    columns = [total[t * rows : (t + 1) * rows] for t in range(2 * tiles)]
    newest = (jnp.concatenate(columns[:tiles], axis=1) * scale).astype(BF).astype(F32)
    gate = (jnp.concatenate(columns[tiles:], axis=1) * scale).astype(BF).astype(F32)
    gate_ref[...] = jax.nn.silu(gate)
    conv = newest * taps_ref[3:4, :]
    for k in range(3):
        conv = conv + state_ref[k].astype(F32) * taps_ref[k : k + 1, :]
    activated = jax.nn.silu(conv + bias_ref[...]).astype(BF)
    act_ref[...] = activated
    part = lax.dot_general(
        activated, proj_ref[...], (((1,), (1,)), ((), ())), preferred_element_type=F32
    )
    half = part.shape[0] // 2
    first = lax.axis_index("side") == 0
    own_ref[...] = jnp.where(first, part[:half], part[half:])
    other_ref[...] = jnp.where(first, part[half:], part[:half])


def state_kernel(
    own_ref, other_ref, act_ref, gate_ref, w_ref, bias_ref, decay_ref, skip_ref, old_ref, new_ref, out_ref, step_ref, scan_ref
):
    rows, width = act_ref.shape
    first = lax.axis_index("side") == 0
    own, other = own_ref[...], other_ref[...]
    params = jnp.concatenate([jnp.where(first, own, other), jnp.where(first, other, own)], axis=0)
    raw = dot(params[:, :RANK].astype(BF), w_ref[...]) + bias_ref[...]
    step_ref[...] = jnp.maximum(raw, 0.0) + jnp.log1p(jnp.exp(-jnp.abs(raw)))
    act = act_ref[...].astype(F32)
    ends = jnp.concatenate([params[:, RANK:], jnp.zeros((rows, 128 - 2 * NSTATE), F32)], axis=1).T
    rate = -jnp.exp(decay_ref[...])
    for r in range(rows):
        step = step_ref[r : r + 1, :]
        entry = ends[:NSTATE, r : r + 1]
        readout = ends[NSTATE : 2 * NSTATE, r : r + 1]
        state = jnp.exp(step * rate) * old_ref[r] + (step * act[r : r + 1, :]) * entry
        new_ref[r] = state
        scan_ref[r : r + 1, :] = jnp.sum(state * readout, axis=0, keepdims=True)
    gated = ((scan_ref[...] + skip_ref[...] * act) * gate_ref[...]).astype(BF)
    for s in range(out_ref.shape[0]):
        out_ref[s] = gated


def join_kernel(a_ref, b_ref, out_ref):
    joined = (a_ref[...] + b_ref[...]).astype(BF)
    for z in range(out_ref.shape[0]):
        out_ref[z] = joined


def mixer_out(x_ref, w_ref, part):
    groups, rows, width = x_ref.shape
    half = groups // 2
    return dot(x_ref[pl.ds(part * half, half)].reshape(half * rows, width), w_ref[...])


def other_out_kernel(x_ref, w_ref, out_ref):
    out_ref[...] = mixer_out(x_ref, w_ref, 1 - lax.axis_index("side")).astype(BF)


def own_out_kernel(x_ref, w_ref, out_ref):
    out_ref[...] = mixer_out(x_ref, w_ref, lax.axis_index("side"))


def add_kernel(a_ref, b_ref, out_ref):
    joined = a_ref[...] + b_ref[...].astype(F32)
    out_ref[...] = joined.astype(BF).reshape(out_ref.shape)


def middle_kernel(x_ref, stream_ref, gain_ref, middle_ref, out_ref):
    middle = stream_ref[...].astype(F32) + jnp.sum(x_ref[...].astype(F32), axis=0)
    middle_ref[...] = middle
    scaled = (middle * gain_ref[...]).astype(BF)
    for z in range(out_ref.shape[0]):
        out_ref[z] = scaled


def tables_kernel(routes_ref, weights_ref, place_ref, mixing_ref, place_t_ref):
    requests = routes_ref.shape[1]
    block = REQ_DEV
    half = requests // 2
    early = lax.broadcasted_iota(jnp.int32, (requests, requests), 0)
    late = lax.broadcasted_iota(jnp.int32, (requests, requests), 1)
    upto = ((early // block == late // block) & (early <= late)).astype(F32).astype(BF)

    expert = lax.broadcasted_iota(jnp.int32, (EXPERTS, requests), 0)
    one = routes_ref[0:1, :] == expert
    two = routes_ref[1:2, :] == expert
    mixing_ref[...] = jnp.where(one, weights_ref[0:1, :], F32(0.0)) + jnp.where(two, weights_ref[1:2, :], F32(0.0))
    hits = (one | two).astype(F32)
    slot = dot(hits.astype(BF), upto).astype(jnp.int32) - 1
    request = lax.broadcasted_iota(jnp.int32, (EXPERTS, requests), 1)
    place = jnp.where(one | two, slot + (request % half) // block * CAP, -1)
    place_ref[...] = place
    wide = jnp.concatenate([place, jnp.zeros((128 - EXPERTS, requests), jnp.int32)], axis=0)
    place_t_ref[...] = wide.T


def dispatch_kernel(x_ref, place_ref, out_ref):
    shards, rows, depth = x_ref.shape
    slots = out_ref.shape[1]
    dense = x_ref[...].reshape(shards * rows, depth)
    place = jnp.where(lax.axis_index("side") == 0, place_ref[:, : shards * rows], place_ref[:, shards * rows :])
    slot = lax.broadcasted_iota(jnp.int32, (slots, shards * rows), 0)
    for e in range(EXPERTS):
        select = (slot == place[e : e + 1, :]).astype(F32).astype(BF)
        picked = dot(select, dense).astype(BF)
        out_ref[2 * e] = picked
        out_ref[2 * e + 1] = picked


def hidden_kernel(x_ref, inverse_ref, g_ref, u_ref, out_ref):
    groups, slots, depth = x_ref.shape
    gate = jnp.zeros((slots, g_ref.shape[2]), F32)
    upper = jnp.zeros((slots, g_ref.shape[2]), F32)
    squares = jnp.zeros((slots, 1), F32)
    for s in range(groups):
        span = slice(s * depth, (s + 1) * depth)
        block = x_ref[s]
        gate = gate + dot(block, g_ref[0, span, :])
        upper = upper + dot(block, u_ref[0, span, :])
        plain = block.astype(F32) * inverse_ref[s : s + 1, :]
        squares = squares + jnp.sum(plain * plain, axis=1, keepdims=True)
    scale = lax.rsqrt(squares / D + EPS)
    out_ref[...] = (jax.nn.silu(gate * scale) * (upper * scale)).astype(BF)


def slot_weight(slots, place_ref, mixing_ref):
    half = place_ref.shape[1] // 2
    expert = lax.axis_index("grp") // 2
    first = lax.axis_index("side") == 0
    row = lax.broadcasted_iota(jnp.int32, place_ref.shape, 0) == expert
    place = jnp.sum(jnp.where(row, place_ref[...], 0), axis=0, keepdims=True)
    mixing = jnp.sum(jnp.where(row, mixing_ref[...], F32(0.0)), axis=0, keepdims=True)
    place = jnp.where(first, place[:, :half], place[:, half:])
    mixing = jnp.where(first, mixing[:, :half], mixing[:, half:])
    slot = lax.broadcasted_iota(jnp.int32, (slots, half), 0)
    return jnp.sum(jnp.where(slot == place, mixing, F32(0.0)), axis=1, keepdims=True)


def down_kernel(own_ref, other_ref, place_ref, mixing_ref, own_d_ref, other_d_ref, out_ref):
    groups, slots, depth = out_ref.shape
    own, other = own_ref[...], other_ref[...]
    weight = slot_weight(slots, place_ref, mixing_ref)
    for s in range(groups):
        span = slice(s * depth, (s + 1) * depth)
        part = dot(own, own_d_ref[0, :, span]) + dot(other, other_d_ref[0, :, span])
        out_ref[s] = (part * weight).astype(BF)


def combine_kernel(x_ref, place_ref, out_ref):
    shards, rows, depth = out_ref.shape
    slots = x_ref.shape[1]
    half = shards * rows
    place = jnp.where(lax.axis_index("side") == 0, place_ref[:half, :], place_ref[half:, :])
    slot = lax.broadcasted_iota(jnp.int32, (half, slots), 1)
    total = jnp.zeros((half, depth), F32)
    for e in range(EXPERTS):
        select = (slot == place[:, e : e + 1]).astype(F32).astype(BF)
        total = total + dot(select, x_ref[2 * e])
        total = total + dot(select, x_ref[2 * e + 1])
    out_ref[...] = total.astype(BF).reshape(shards, rows, depth)


def sum_kernel(x_ref, out_ref):
    out_ref[...] = jnp.sum(x_ref[...].astype(F32), axis=0)


def final_kernel(x_ref, middle_ref, out_ref):
    out_ref[...] = (middle_ref[...] + jnp.sum(x_ref[...].astype(F32), axis=0)).astype(BF)


def local(
    stream,
    mixer_gain,
    in_weight,
    conv_state,
    conv_weight,
    conv_bias,
    proj_weight,
    step_weight,
    step_bias,
    decay_log,
    skip_gain,
    ssm_state,
    out_weight,
    moe_gain,
    routes,
    route_weight,
    gate_weight,
    up_weight,
    down_weight,
):
    groups = lax.axis_size("grp")
    shards = lax.axis_size("shard")
    rows, slice_width = stream.shape
    width = in_weight.shape[2]
    side_rows = shards * rows
    slots = shards * CAP

    packet = jnp.broadcast_to(stream[None], (shards, rows, slice_width))
    gains = jnp.stack([mixer_gain, moe_gain])
    near = exchange(packet, "shard")
    far = swap(near)

    (packet,) = on_core(
        project_kernel,
        [((groups, 2 * width // 128 * rows + 16, 128), BF)],
        near,
        far,
        gains,
        in_weight.reshape(slice_width, 2 * width),
    )
    packet, *sent = lax.optimization_barrier((packet, gate_weight, up_weight, down_weight))
    other_gate, other_up, other_down = [swap(weight) for weight in sent]
    arrived = exchange(packet, "grp")
    some = (rows // 2, proj_weight.shape[0])
    activated, gate, own, other, inverse = on_core(
        conv_kernel,
        [((rows, width), BF), ((rows, width), F32), (some, F32), (some, F32), ((groups, slice_width), F32)],
        arrived,
        conv_state.transpose(1, 0, 2),
        conv_weight,
        conv_bias[None],
        proj_weight,
    )

    listed, listed_weight, own = lax.optimization_barrier((routes.T, route_weight.T, own))
    requests = routes.shape[0]
    place, mixing, place_t = on_core(
        tables_kernel,
        [((EXPERTS, requests), jnp.int32), ((EXPERTS, requests), F32), ((requests, 128), jnp.int32)],
        listed,
        listed_weight,
    )
    own, place, mixing, place_t = lax.optimization_barrier((own, place, mixing, place_t))

    (packet,) = on_core(join_kernel, [((shards,) + some, BF)], own, swap(other))
    (own,) = on_core(sum_kernel, [(some, F32)], exchange(packet, "shard"))
    new_state, packet = on_core(
        state_kernel,
        [(ssm_state.shape, F32), ((groups, rows, width), BF)],
        own,
        swap(own),
        activated,
        gate,
        step_weight,
        step_bias[None],
        decay_log,
        skip_gain[None],
        ssm_state,
        scratch=[pltpu.VMEM((rows, width), F32)] * 2,
    )

    all_gated = exchange(packet, "grp")
    (other,) = on_core(other_out_kernel, [((side_rows, slice_width), BF)], all_gated, out_weight)
    (own,) = on_core(own_out_kernel, [((side_rows, slice_width), F32)], all_gated, out_weight)
    (packet,) = on_core(add_kernel, [((shards, rows, slice_width), BF)], own, swap(other))
    middle, packet = on_core(
        middle_kernel,
        [((rows, slice_width), F32), ((shards, rows, slice_width), BF)],
        exchange(packet, "shard"),
        stream,
        moe_gain[None],
    )
    dense = exchange(packet, "shard")

    (packet,) = on_core(dispatch_kernel, [((groups, slots, slice_width), BF)], dense, place)
    packet, other_gate, other_up, other_down = lax.optimization_barrier((packet, other_gate, other_up, other_down))
    arrived = exchange(packet, "grp")

    work = 2 * slots * D * gate_weight.shape[2]
    some = [((slots, gate_weight.shape[2]), BF)]
    (own,) = on_core(hidden_kernel, some, arrived, inverse, gate_weight, up_weight, flops=2 * work)
    (other,) = on_core(hidden_kernel, some, arrived, inverse, other_gate, other_up, flops=2 * work)
    (packet,) = on_core(
        down_kernel,
        [((groups, slots, slice_width), BF)],
        own,
        other,
        place,
        mixing,
        down_weight,
        other_down,
        flops=2 * work,
    )
    back = exchange(packet, "grp")

    (packet,) = on_core(combine_kernel, [((shards, rows, slice_width), BF)], back, place_t)
    (mixed,) = on_core(final_kernel, [((rows, slice_width), BF)], exchange(packet, "shard"), middle)
    return (mixed, new_state)


def solution(mesh):
    placed = (
        P(("side", "shard"), "grp"),
        P("grp"),
        P("grp", None, ("side", "shard")),
        P("grp", None, ("side", "shard")),
        P(None, ("side", "shard")),
        P(("side", "shard")),
        P(None, ("side", "shard")),
        P(None, ("side", "shard")),
        P(("side", "shard")),
        P(None, ("side", "shard")),
        P(("side", "shard")),
        P("grp", None, ("side", "shard")),
        P(("side", "shard"), "grp"),
        P("grp"),
        P(),
        P(),
        P("grp", None, ("side", "shard")),
        P("grp", None, ("side", "shard")),
        P("grp", ("side", "shard"), None),
    )
    return jax.shard_map(
        local,
        mesh=mesh,
        in_specs=placed,
        out_specs=(P(("side", "shard"), "grp"), P("grp", None, ("side", "shard"))),
        check_vma=False,
    )
```

```python
import math

import jax
import jax.numpy as jnp
from jax import lax
from jax.experimental import pallas as pl
from jax.experimental.pallas import tpu as pltpu
from jax.sharding import PartitionSpec as P

D = 4096
NSTATE = 16
RANK = 512
EXPERTS = 8
CAP = 20
REQ_DEV = 32
EPS = 1e-06
BF = jnp.bfloat16
F32 = jnp.float32


def on_core(kernel, outs, *operands, scratch=(), flops=0, limit=0):
    vmem = pl.BlockSpec(memory_space=pltpu.VMEM)
    moved = sum(o.size * o.dtype.itemsize for o in operands)
    limit = limit or moved + sum(math.prod(s) * jnp.dtype(d).itemsize for s, d in outs) + 3 * 2**20
    return pl.pallas_call(
        kernel,
        out_shape=[jax.ShapeDtypeStruct(s, d) for s, d in outs],
        in_specs=[vmem] * len(operands),
        out_specs=[vmem] * len(outs),
        scratch_shapes=scratch,
        compiler_params=pltpu.CompilerParams(vmem_limit_bytes=limit),
        cost_estimate=pl.CostEstimate(flops=flops, bytes_accessed=moved, transcendentals=0),
    )(*operands)


def dot(a, b):
    return jnp.dot(a, b, preferred_element_type=F32)


def split_wide(values):
    high = values.astype(BF)
    low = (values - high.astype(F32)).astype(BF)
    return high, low


def swap(block):
    return lax.ppermute(block, "side", [(0, 1), (1, 0)])


def exchange(block, axis):
    return lax.all_to_all(block, axis, 0, 0)


def spread(block, axis):
    count = lax.axis_size(axis)
    return exchange(jnp.broadcast_to(block[None], (count,) + block.shape), axis)


def project_kernel(near_ref, far_ref, gains_ref, w_ref, out_ref):
    shards, rows, depth = near_ref.shape
    tiles = w_ref.shape[1] // 128
    side = lax.axis_index("side")
    same = lax.broadcasted_iota(jnp.int32, (rows, 128), 0) == lax.broadcasted_iota(jnp.int32, (rows, 128), 1)
    row = lax.broadcasted_iota(jnp.int32, (16, 128), 0)
    gain = gains_ref[1:2, :]
    high = gain.astype(BF).astype(F32)
    mid = (gain - high).astype(BF).astype(F32)
    low = gain - high - mid
    tail = jnp.zeros((16, 128), F32)
    for k, term in enumerate((high, mid, low)):
        for h in range(depth // 128):
            tail = jnp.where(row == 2 + 2 * k + h, term[:, h * 128 : (h + 1) * 128], tail)
    for block_ref, c in ((near_ref, side), (far_ref, 1 - side)):
        wide = block_ref[...].reshape(shards * rows, depth).astype(F32)
        squares = jnp.sum(wide * wide, axis=1, keepdims=True)
        part = dot((wide * gains_ref[0:1, :]).astype(BF), w_ref[...])
        for z in range(shards):
            span = slice(z * rows, (z + 1) * rows)
            for t in range(tiles):
                out_ref[c * shards + z, t * rows : (t + 1) * rows, :] = part[span, t * 128 : (t + 1) * 128].astype(BF)
            across = jnp.sum(jnp.where(same, squares[span], F32(0.0)), axis=0, keepdims=True)
            high = across.astype(BF).astype(F32)
            extra = jnp.where(row == 0, high, jnp.where(row == 1, across - high, tail))
            out_ref[c * shards + z, tiles * rows :, :] = extra.astype(BF)


def conv_kernel(
    x_ref, state_ref, taps_ref, bias_ref, proj_ref, act_ref, gate_ref, own_ref, other_ref, inverse_ref
):
    rows, width = act_ref.shape
    tiles = width // 128
    total = jnp.sum(x_ref[...].astype(F32), axis=0)
    end = 2 * tiles * rows
    across = total[end : end + 1] + total[end + 1 : end + 2]
    same = lax.broadcasted_iota(jnp.int32, (rows, 128), 0) == lax.broadcasted_iota(jnp.int32, (rows, 128), 1)
    squares = jnp.sum(jnp.where(same, across, F32(0.0)), axis=1, keepdims=True)
    scale = lax.rsqrt(squares / D + EPS)
    for s in range(x_ref.shape[0]):
        extra = x_ref[s, end:, :].astype(F32)
        for h in range(inverse_ref.shape[1] // 128):
            gain = extra[2 + h : 3 + h] + extra[4 + h : 5 + h] + extra[6 + h : 7 + h]
            inverse_ref[s : s + 1, h * 128 : (h + 1) * 128] = 1.0 / gain
    columns = [total[t * rows : (t + 1) * rows] for t in range(2 * tiles)]
    newest = (jnp.concatenate(columns[:tiles], axis=1) * scale).astype(BF).astype(F32)
    gate = (jnp.concatenate(columns[tiles:], axis=1) * scale).astype(BF).astype(F32)
    gate_ref[...] = jax.nn.silu(gate)
    conv = newest * taps_ref[3:4, :]
    for k in range(3):
        conv = conv + state_ref[k].astype(F32) * taps_ref[k : k + 1, :]
    activated = jax.nn.silu(conv + bias_ref[...]).astype(BF)
    act_ref[...] = activated
    part = lax.dot_general(
        activated, proj_ref[...], (((1,), (1,)), ((), ())), preferred_element_type=F32
    )
    half = part.shape[0] // 2
    first = lax.axis_index("side") == 0
    own_ref[...] = jnp.where(first, part[:half], part[half:])
    other_ref[...] = jnp.where(first, part[half:], part[:half])


def state_kernel(
    own_ref, other_ref, act_ref, gate_ref, w_ref, bias_ref, decay_ref, skip_ref, old_ref, new_ref, out_ref, step_ref, scan_ref
):
    rows, width = act_ref.shape
    first = lax.axis_index("side") == 0
    own, other = own_ref[...], other_ref[...]
    params = jnp.concatenate([jnp.where(first, own, other), jnp.where(first, other, own)], axis=0)
    raw = dot(params[:, :RANK].astype(BF), w_ref[...]) + bias_ref[...]
    step_ref[...] = jnp.maximum(raw, 0.0) + jnp.log1p(jnp.exp(-jnp.abs(raw)))
    act = act_ref[...].astype(F32)
    ends = jnp.concatenate([params[:, RANK:], jnp.zeros((rows, 128 - 2 * NSTATE), F32)], axis=1).T
    rate = -jnp.exp(decay_ref[...])
    for r in range(rows):
        step = step_ref[r : r + 1, :]
        entry = ends[:NSTATE, r : r + 1]
        readout = ends[NSTATE : 2 * NSTATE, r : r + 1]
        state = jnp.exp(step * rate) * old_ref[r] + (step * act[r : r + 1, :]) * entry
        new_ref[r] = state
        scan_ref[r : r + 1, :] = jnp.sum(state * readout, axis=0, keepdims=True)
    gated = ((scan_ref[...] + skip_ref[...] * act) * gate_ref[...]).astype(BF)
    for s in range(out_ref.shape[0]):
        out_ref[s] = gated


def join_kernel(a_ref, b_ref, out_ref):
    rows = a_ref.shape[0]
    joined = a_ref[...] + b_ref[...]
    tiles = [joined[:, t * 128 : (t + 1) * 128] for t in range(RANK // 128)]
    last = joined[:, RANK:]
    quarter = rows // 4
    tail = jnp.concatenate([last[q * quarter : (q + 1) * quarter] for q in range(4)], axis=1)
    packed = jnp.concatenate(tiles + [tail, jnp.zeros((8 - quarter, 128), F32)], axis=0).astype(BF)
    for z in range(out_ref.shape[0]):
        out_ref[z] = packed


def mixer_out(x_ref, w_ref, part):
    groups, rows, width = x_ref.shape
    half = groups // 2
    return dot(x_ref[pl.ds(part * half, half)].reshape(half * rows, width), w_ref[...])


def other_out_kernel(x_ref, w_ref, out_ref):
    out_ref[...] = mixer_out(x_ref, w_ref, 1 - lax.axis_index("side")).astype(BF)


def own_out_kernel(x_ref, w_ref, out_ref):
    out_ref[...] = mixer_out(x_ref, w_ref, lax.axis_index("side"))


def add_kernel(a_ref, b_ref, out_ref):
    joined = a_ref[...] + b_ref[...].astype(F32)
    out_ref[...] = joined.astype(BF).reshape(out_ref.shape)


def middle_kernel(x_ref, stream_ref, gain_ref, middle_ref, out_ref):
    middle = stream_ref[...].astype(F32) + jnp.sum(x_ref[...].astype(F32), axis=0)
    middle_ref[...] = middle
    scaled = (middle * gain_ref[...]).astype(BF)
    for z in range(out_ref.shape[0]):
        out_ref[z] = scaled


def tables_kernel(routes_ref, weights_ref, place_ref, mixing_ref, place_t_ref):
    requests = routes_ref.shape[1]
    block = REQ_DEV
    half = requests // 2
    early = lax.broadcasted_iota(jnp.int32, (requests, requests), 0)
    late = lax.broadcasted_iota(jnp.int32, (requests, requests), 1)
    upto = ((early // block == late // block) & (early <= late)).astype(F32).astype(BF)

    expert = lax.broadcasted_iota(jnp.int32, (EXPERTS, requests), 0)
    one = routes_ref[0:1, :] == expert
    two = routes_ref[1:2, :] == expert
    mixing_ref[...] = jnp.where(one, weights_ref[0:1, :], F32(0.0)) + jnp.where(two, weights_ref[1:2, :], F32(0.0))
    hits = (one | two).astype(F32)
    slot = dot(hits.astype(BF), upto).astype(jnp.int32) - 1
    request = lax.broadcasted_iota(jnp.int32, (EXPERTS, requests), 1)
    place = jnp.where(one | two, slot + (request % half) // block * CAP, -1)
    place_ref[...] = place
    wide = jnp.concatenate([place, jnp.zeros((128 - EXPERTS, requests), jnp.int32)], axis=0)
    place_t_ref[...] = wide.T


def dispatch_kernel(x_ref, place_ref, out_ref):
    shards, rows, depth = x_ref.shape
    slots = out_ref.shape[1]
    dense = x_ref[...].reshape(shards * rows, depth)
    place = jnp.where(lax.axis_index("side") == 0, place_ref[:, : shards * rows], place_ref[:, shards * rows :])
    slot = lax.broadcasted_iota(jnp.int32, (slots, shards * rows), 0)
    for e in range(EXPERTS):
        select = (slot == place[e : e + 1, :]).astype(F32).astype(BF)
        picked = dot(select, dense).astype(BF)
        out_ref[2 * e] = picked
        out_ref[2 * e + 1] = picked


def hidden_kernel(x_ref, inverse_ref, g_ref, u_ref, out_ref):
    groups, slots, depth = x_ref.shape
    gate = jnp.zeros((slots, g_ref.shape[2]), F32)
    upper = jnp.zeros((slots, g_ref.shape[2]), F32)
    squares = jnp.zeros((slots, 1), F32)
    for s in range(groups):
        span = slice(s * depth, (s + 1) * depth)
        block = x_ref[s]
        gate = gate + dot(block, g_ref[0, span, :])
        upper = upper + dot(block, u_ref[0, span, :])
        plain = block.astype(F32) * inverse_ref[s : s + 1, :]
        squares = squares + jnp.sum(plain * plain, axis=1, keepdims=True)
    scale = lax.rsqrt(squares / D + EPS)
    out_ref[...] = (jax.nn.silu(gate * scale) * (upper * scale)).astype(BF)


def slot_weight(slots, place_ref, mixing_ref):
    half = place_ref.shape[1] // 2
    expert = lax.axis_index("grp") // 2
    first = lax.axis_index("side") == 0
    row = lax.broadcasted_iota(jnp.int32, place_ref.shape, 0) == expert
    place = jnp.sum(jnp.where(row, place_ref[...], 0), axis=0, keepdims=True)
    mixing = jnp.sum(jnp.where(row, mixing_ref[...], F32(0.0)), axis=0, keepdims=True)
    place = jnp.where(first, place[:, :half], place[:, half:])
    mixing = jnp.where(first, mixing[:, :half], mixing[:, half:])
    slot = lax.broadcasted_iota(jnp.int32, (slots, half), 0)
    return jnp.sum(jnp.where(slot == place, mixing, F32(0.0)), axis=1, keepdims=True)


def down_kernel(own_ref, other_ref, place_ref, mixing_ref, own_d_ref, other_d_ref, out_ref):
    groups, slots, depth = out_ref.shape
    own, other = own_ref[...], other_ref[...]
    weight = slot_weight(slots, place_ref, mixing_ref)
    for s in range(groups):
        span = slice(s * depth, (s + 1) * depth)
        part = dot(own, own_d_ref[0, :, span]) + dot(other, other_d_ref[0, :, span])
        out_ref[s] = (part * weight).astype(BF)


def combine_kernel(x_ref, place_ref, out_ref):
    shards, rows, depth = out_ref.shape
    slots = x_ref.shape[1]
    half = shards * rows
    place = jnp.where(lax.axis_index("side") == 0, place_ref[:half, :], place_ref[half:, :])
    slot = lax.broadcasted_iota(jnp.int32, (half, slots), 1)
    total = jnp.zeros((half, depth), F32)
    for e in range(EXPERTS):
        select = (slot == place[:, e : e + 1]).astype(F32).astype(BF)
        total = total + dot(select, x_ref[2 * e])
        total = total + dot(select, x_ref[2 * e + 1])
    out_ref[...] = total.astype(BF).reshape(shards, rows, depth)


def sum_kernel(x_ref, out_ref):
    rows = out_ref.shape[0]
    quarter = rows // 4
    total = jnp.sum(x_ref[...].astype(F32), axis=0)
    end = RANK // 128 * rows
    for t in range(RANK // 128):
        out_ref[:, t * 128 : (t + 1) * 128] = total[t * rows : (t + 1) * rows]
    tail = total[end : end + quarter]
    out_ref[:, RANK:] = jnp.concatenate([tail[:, q * 32 : (q + 1) * 32] for q in range(4)], axis=0)


def final_kernel(x_ref, middle_ref, out_ref):
    out_ref[...] = (middle_ref[...] + jnp.sum(x_ref[...].astype(F32), axis=0)).astype(BF)


def local(
    stream,
    mixer_gain,
    in_weight,
    conv_state,
    conv_weight,
    conv_bias,
    proj_weight,
    step_weight,
    step_bias,
    decay_log,
    skip_gain,
    ssm_state,
    out_weight,
    moe_gain,
    routes,
    route_weight,
    gate_weight,
    up_weight,
    down_weight,
):
    groups = lax.axis_size("grp")
    shards = lax.axis_size("shard")
    rows, slice_width = stream.shape
    width = in_weight.shape[2]
    side_rows = shards * rows
    slots = shards * CAP

    packet = jnp.broadcast_to(stream[None], (shards, rows, slice_width))
    gains = jnp.stack([mixer_gain, moe_gain])
    near = exchange(packet, "shard")
    far = swap(near)

    (packet,) = on_core(
        project_kernel,
        [((groups, 2 * width // 128 * rows + 16, 128), BF)],
        near,
        far,
        gains,
        in_weight.reshape(slice_width, 2 * width),
    )
    packet, *sent = lax.optimization_barrier((packet, gate_weight, up_weight, down_weight))
    other_gate, other_up, other_down = [swap(weight) for weight in sent]
    arrived = exchange(packet, "grp")
    some = (rows // 2, proj_weight.shape[0])
    activated, gate, own, other, inverse = on_core(
        conv_kernel,
        [((rows, width), BF), ((rows, width), F32), (some, F32), (some, F32), ((groups, slice_width), F32)],
        arrived,
        conv_state.transpose(1, 0, 2),
        conv_weight,
        conv_bias[None],
        proj_weight,
    )

    listed, listed_weight, own = lax.optimization_barrier((routes.T, route_weight.T, own))
    requests = routes.shape[0]
    place, mixing, place_t = on_core(
        tables_kernel,
        [((EXPERTS, requests), jnp.int32), ((EXPERTS, requests), F32), ((requests, 128), jnp.int32)],
        listed,
        listed_weight,
    )
    own, place, mixing, place_t = lax.optimization_barrier((own, place, mixing, place_t))

    (packet,) = on_core(join_kernel, [((shards, RANK // 128 * rows // 2 + 8, 128), BF)], own, swap(other))
    (own,) = on_core(sum_kernel, [(some, F32)], exchange(packet, "shard"))
    new_state, packet = on_core(
        state_kernel,
        [(ssm_state.shape, F32), ((groups, rows, width), BF)],
        own,
        swap(own),
        activated,
        gate,
        step_weight,
        step_bias[None],
        decay_log,
        skip_gain[None],
        ssm_state,
        scratch=[pltpu.VMEM((rows, width), F32)] * 2,
    )

    all_gated = exchange(packet, "grp")
    (other,) = on_core(other_out_kernel, [((side_rows, slice_width), BF)], all_gated, out_weight)
    (own,) = on_core(own_out_kernel, [((side_rows, slice_width), F32)], all_gated, out_weight)
    (packet,) = on_core(add_kernel, [((shards, rows, slice_width), BF)], own, swap(other))
    middle, packet = on_core(
        middle_kernel,
        [((rows, slice_width), F32), ((shards, rows, slice_width), BF)],
        exchange(packet, "shard"),
        stream,
        moe_gain[None],
    )
    dense = exchange(packet, "shard")

    (packet,) = on_core(dispatch_kernel, [((groups, slots, slice_width), BF)], dense, place)
    packet, other_gate, other_up, other_down = lax.optimization_barrier((packet, other_gate, other_up, other_down))
    arrived = exchange(packet, "grp")

    work = 2 * slots * D * gate_weight.shape[2]
    some = [((slots, gate_weight.shape[2]), BF)]
    (own,) = on_core(hidden_kernel, some, arrived, inverse, gate_weight, up_weight, flops=2 * work)
    (other,) = on_core(hidden_kernel, some, arrived, inverse, other_gate, other_up, flops=2 * work)
    (packet,) = on_core(
        down_kernel,
        [((groups, slots, slice_width), BF)],
        own,
        other,
        place,
        mixing,
        down_weight,
        other_down,
        flops=2 * work,
    )
    back = exchange(packet, "grp")

    (packet,) = on_core(combine_kernel, [((shards, rows, slice_width), BF)], back, place_t)
    (mixed,) = on_core(final_kernel, [((rows, slice_width), BF)], exchange(packet, "shard"), middle)
    return (mixed, new_state)


def solution(mesh):
    placed = (
        P(("side", "shard"), "grp"),
        P("grp"),
        P("grp", None, ("side", "shard")),
        P("grp", None, ("side", "shard")),
        P(None, ("side", "shard")),
        P(("side", "shard")),
        P(None, ("side", "shard")),
        P(None, ("side", "shard")),
        P(("side", "shard")),
        P(None, ("side", "shard")),
        P(("side", "shard")),
        P("grp", None, ("side", "shard")),
        P(("side", "shard"), "grp"),
        P("grp"),
        P(),
        P(),
        P("grp", None, ("side", "shard")),
        P("grp", None, ("side", "shard")),
        P("grp", ("side", "shard"), None),
    )
    return jax.shard_map(
        local,
        mesh=mesh,
        in_specs=placed,
        out_specs=(P(("side", "shard"), "grp"), P("grp", None, ("side", "shard"))),
        check_vma=False,
    )
```
